256 devices in a mesh: dp: 8 (over y, core), shard: 32 (over z, x).
Axes of the slice: x: 4, y: 4, z: 8, core: 2. Of those that a mesh axis runs over, the one named last changes fastest.
Arguments:
- grads: bfloat16 [104, 1024, 704], P(None, 'shard'), may hold values from -150 to 150
- momentum: bfloat16 [256, 1024, 704], P(('dp', 'shard')), may hold values from -24 to 24
- owners: int32 [104], replicated, may hold values from 0 to 255, as said below
Outputs:
- updates: bfloat16 [104, 1024, 704], P(None, 'shard')
- momentum_next: bfloat16 [256, 1024, 704], P(('dp', 'shard'))
The draws below stay inside these ranges and needn't reach their ends.
Inputs may be any that keep to these rules, and one draw needn't show every extreme that they name: `owners`: device d is the one with dp index d // 32 and shard index d % 32. Each device owns at most 1 matrices, and some device owns exactly 1.
All inputs are finite; a program needn't handle non-finite values.
Results may differ from the reference program's by a relative error of at most 0.0058.
Values may be sent and summed in bfloat16 or wider, within the bound.
No kernel may reach another device: no remote copies, remote signals or barrier semaphores. Data moves between devices by JAX's collectives and lax.ppermute only.
A program may use at most 128 MiB of HBM per device.

```python
import math
import jax
import jax.numpy as jnp
from jax import lax

R = 1024
C = 704
ITERS = 2
OWN_MOST = 1
MAT_GROUP = 13
SLOTS = 256
N_DP = 8
N_SHARD = 32


def draw_grads(key, part):
    key = jax.random.fold_in(key, 5)
    key_base, key_rows, key_cols = jax.random.split(key, 3)
    full_shape = (MAT_GROUP * N_DP, R, C)
    base_values = jnp.clip(jax.random.normal(key_base, full_shape, jnp.float32), -6.0, 6.0)
    row_scale = jnp.exp(jax.random.uniform(key_rows, (MAT_GROUP * N_DP, R, 1), jnp.float32, 0.0, math.log(10.0)))
    col_scale = jnp.exp(jax.random.uniform(key_cols, (MAT_GROUP * N_DP, 1, C), jnp.float32, 0.0, math.log(10.0)))
    return (0.25 * base_values * row_scale * col_scale).astype(jnp.bfloat16)


def draw_owners(key, part):
    key = jax.random.fold_in(key, 9)
    seat_count = OWN_MOST * N_DP * N_SHARD
    seats = jax.random.permutation(key, seat_count).astype(jnp.int32)
    partner = seats[0] // OWN_MOST * OWN_MOST + (seats[0] + 1) % OWN_MOST
    location = jnp.argmax(seats == partner)
    moved = seats.at[location].set(seats[1]).at[1].set(partner)
    return (moved[:MAT_GROUP * N_DP] // OWN_MOST).astype(jnp.int32)


def steps_of(key, shape, cuts, smallest, high):
    level = 1.0
    for position, blocks in cuts:
        steps = jax.random.uniform(jax.random.fold_in(jax.random.fold_in(key, 6), position), (blocks,), jnp.float32, smallest / len(cuts), high / len(cuts))
        level = level * jnp.repeat(jnp.exp(steps), shape[position] // blocks).reshape((-1,) + (1,) * (len(shape) - 1 - position))
    return level


def centred(own_key, shape, spread, bound, shards=(), kind=jnp.bfloat16):
    level = steps_of(own_key, shape, shards, -0.22, 0.18) if shards else 1.0
    values = jax.random.normal(own_key, shape, jnp.float32) * spread * level
    return jnp.minimum(jnp.maximum(values, -bound), bound).astype(kind)


def setup_inputs(seed: int = 0) -> dict:
    streams_of = jax.random.split(jax.random.key(seed), 4)
    return {
        "grads": draw_grads(jax.random.fold_in(streams_of[3], 71), 0),
        "momentum": centred(streams_of[1], (SLOTS, R, C), 4.0, 24.0, ((0, 256),)),
        "owners": draw_owners(jax.random.fold_in(streams_of[3], 71), 0),
    }


momentum_decay = 0.95
coeff_linear = 3.4445
coeff_cubic = -4.775
coeff_quintic = 2.0315
norm_eps = 1e-07

def ranks_of(owners):
    count = owners.shape[0]
    positions = jnp.arange(count, dtype=jnp.int32)
    same_owner = owners[:, None] == owners[None, :]
    earlier = positions[None, :] < positions[:, None]
    return lax.optimization_barrier(jnp.sum((same_owner & earlier).astype(jnp.int32), axis=1)).astype(jnp.int32)

def orthogonalize(start):
    current = start
    following = start.astype(jnp.float32)
    for iteration in range(ITERS):
        gram_matrix = jnp.dot(current.T, current, preferred_element_type=jnp.float32).astype(jnp.bfloat16)
        square = jnp.dot(gram_matrix, gram_matrix, preferred_element_type=jnp.float32)
        polynomial = (coeff_cubic * gram_matrix.astype(jnp.float32) + coeff_quintic * square).astype(jnp.bfloat16)
        following = coeff_linear * current.astype(jnp.float32) + jnp.dot(current, polynomial, preferred_element_type=jnp.float32)
        if iteration + 1 < ITERS:
            current = following.astype(jnp.bfloat16)
    return following

def orthonormal_update(gradient, renewed):
    blend = gradient + momentum_decay * renewed
    magnitude = jnp.sqrt(jnp.sum(blend * blend))
    start = (blend / (magnitude + norm_eps)).astype(jnp.bfloat16)
    final = orthogonalize(start)
    update_scale = 0.2 * math.sqrt(max(final.shape[0], final.shape[1]))
    return (update_scale * final).astype(jnp.bfloat16)

def reference(grads, momentum, owners):
    ranks = ranks_of(owners)
    slot_index = (owners * OWN_MOST + ranks).astype(jnp.int32)
    picked = momentum[slot_index]

    def one_matrix(pair):
        gradient = pair[0].astype(jnp.float32)
        renewed = momentum_decay * pair[1].astype(jnp.float32) + gradient
        return (renewed.astype(jnp.bfloat16), orthonormal_update(gradient, renewed))
    renewed_all, updates = lax.map(one_matrix, (grads, picked))
    base_momentum = (momentum_decay * momentum.astype(jnp.float32)).astype(jnp.bfloat16)
    momentum_next = base_momentum.at[slot_index].set(renewed_all)
    return (updates, momentum_next)
```

```python
import functools
import math

import jax
import jax.numpy as jnp
from jax import lax
from jax.experimental import pallas as pl
from jax.experimental.pallas import tpu as pltpu
from jax.sharding import PartitionSpec as P

DECAY = 0.95
LINEAR, CUBIC, QUINTIC = 3.4445, -4.775, 2.0315
EPS = 1e-07
ITERS = 2
AXES = ("dp", "shard")
NZ, NX, NC, NY = 8, 4, 2, 4
SHARDS = NZ * NX
RING = NC * SHARDS
NT = (((1,), (1,)), ((), ()))
NN = (((1,), (0,)), ((), ()))
ANY = pl.BlockSpec(memory_space=pl.ANY)
HBM = pl.BlockSpec(memory_space=pltpu.HBM)
SMEM = pl.BlockSpec(memory_space=pltpu.SMEM)
VMEM = pl.BlockSpec(memory_space=pltpu.VMEM)


def seat(z, x):
    pick = jnp.where if isinstance(z, jax.Array) else (lambda c, a, b: a if c else b)
    return pick(z < NZ // 2, 2 * z, 2 * NZ - 1 - 2 * z) + NZ * pick(x < NX // 2, 2 * x, 2 * NX - 1 - 2 * x)


SEATED = sorted(range(SHARDS), key=lambda s: seat(s // NX, s % NX))
GROUPS_32 = [[g * SHARDS + s for s in SEATED] for g in range(NY * NC)]
GROUPS_64 = [[y * RING + c * SHARDS + s for c in range(NC) for s in SEATED] for y in range(NY)]


def hop_y(array, step):
    count = NY * RING
    return lax.ppermute(array, AXES, [(d, (d + RING * step) % count) for d in range(count)])


def hop_core(array):
    return lax.ppermute(array, AXES, [(d, d ^ SHARDS) for d in range(NY * RING)])


def pack_kernel(owners, group, grads, out, sems):
    def copy(m):
        shard = owners[m] % SHARDS
        place = seat(shard // NX, shard % NX)
        return pltpu.make_async_copy(grads.at[m], out.at[place], sems.at[m])

    def start(m, carry):
        pl.when(owners[m] // SHARDS == group[0])(lambda: copy(m).start())
        return carry

    def wait(m, carry):
        pl.when(owners[m] // SHARDS == group[0])(lambda: copy(m).wait())
        return carry

    lax.fori_loop(0, owners.shape[0], start, 0)
    lax.fori_loop(0, owners.shape[0], wait, 0)


def pack(owners, group, grads):
    count, rows, columns = grads.shape
    return pl.pallas_call(
        pack_kernel,
        out_shape=jax.ShapeDtypeStruct((SHARDS, rows, columns), grads.dtype),
        in_specs=[SMEM, SMEM, HBM],
        out_specs=ANY,
        scratch_shapes=[pltpu.SemaphoreType.DMA((count,))],
        name="pack_rows",
    )(owners, group, grads)


def dot(a, b, dims):
    return lax.dot_general(a, b, dims, preferred_element_type=jnp.float32)


def step_kernel(scale, owned_ref, rows_ref, mom_ref, out_ref, next_ref, blend, cur, gram, poly):
    rows = rows_ref.shape[1]
    half = rows // NC
    span = NX * rows
    owned = owned_ref[0] > 0
    total = jnp.zeros((8, span), jnp.float32)
    for z in range(NZ):
        cols = slice(z * span, (z + 1) * span)
        grad = jnp.concatenate([rows_ref[seat(z, x)] for x in range(NX)], axis=0)
        grad = jnp.where(owned, grad.T.astype(jnp.float32), 0.0)
        renewed = DECAY * mom_ref[:, cols].astype(jnp.float32) + grad
        next_ref[:, cols] = renewed.astype(jnp.bfloat16)
        mixed = grad + DECAY * renewed
        blend[:, cols] = mixed
        total = total + jnp.sum((mixed * mixed).reshape(-1, 8, span), axis=0)
    inverse = 1.0 / (jnp.sqrt(jnp.sum(total)) + EPS)
    cur[...] = (blend[...] * inverse).astype(jnp.bfloat16)
    for iteration in range(ITERS):
        x = cur[...]
        gram[...] = dot(x, x, NT).astype(jnp.bfloat16)
        g = gram[...]
        poly[...] = (CUBIC * g.astype(jnp.float32) + QUINTIC * dot(g, g, NN)).astype(jnp.bfloat16)
        if iteration + 1 < ITERS:
            cur[...] = (LINEAR * x.astype(jnp.float32) + dot(poly[...], x, NN)).astype(jnp.bfloat16)
            continue
        for z in range(NZ):
            xz = cur[:, z * span : (z + 1) * span]
            last = LINEAR * xz.astype(jnp.float32) + dot(poly[...], xz, NN)
            update = (scale * last).astype(jnp.bfloat16).T
            for x in range(NX):
                for c in range(NC):
                    low = x * rows + c * half
                    out_ref[c * SHARDS + seat(z, x)] = update[low : low + half]


def muon_step(owned, rows, momentum_t):
    columns, total_rows = momentum_t.shape
    scale = 0.2 * math.sqrt(max(columns, total_rows))
    square = pltpu.VMEM((columns, columns), jnp.bfloat16)
    return pl.pallas_call(
        functools.partial(step_kernel, scale),
        out_shape=(
            jax.ShapeDtypeStruct((RING, rows.shape[1] // NC, columns), jnp.bfloat16),
            jax.ShapeDtypeStruct(momentum_t.shape, jnp.bfloat16),
        ),
        in_specs=[SMEM, VMEM, VMEM],
        out_specs=(VMEM, VMEM),
        scratch_shapes=[
            pltpu.VMEM(momentum_t.shape, jnp.float32),
            pltpu.VMEM(momentum_t.shape, jnp.bfloat16),
            square,
            square,
        ],
        compiler_params=pltpu.CompilerParams(vmem_limit_bytes=48 * 2**20),
        name="newton_schulz",
    )(owned, rows, momentum_t)


def select_kernel(owners, order, counts, where, blocks, out, sems):
    y = where[0]

    def copy(k):
        device = owners[order[y * RING + k]] % RING
        shard = device % SHARDS
        place = device // SHARDS * SHARDS + seat(shard // NX, shard % NX)
        return pltpu.make_async_copy(blocks.at[place], out.at[k], sems.at[k])

    def start(k, carry):
        copy(k).start()
        return carry

    def wait(k, carry):
        copy(k).wait()
        return carry

    lax.fori_loop(0, counts[y], start, 0)
    lax.fori_loop(0, counts[y], wait, 0)


def select(owners, order, counts, where, blocks, slots):
    return pl.pallas_call(
        select_kernel,
        out_shape=jax.ShapeDtypeStruct((slots,) + blocks.shape[1:], blocks.dtype),
        in_specs=[SMEM] * 4 + [ANY],
        out_specs=ANY,
        scratch_shapes=[pltpu.SemaphoreType.DMA((slots,))],
        name="select_blocks",
    )(owners, order, counts, where, blocks)


def place_kernel(order, counts, where, *refs):
    pieces, out, sems = refs[: NC * NY], refs[NC * NY], refs[NC * NY + 1]
    y, c = where[0], where[1]
    half = out.shape[1] // NC
    for run in ("start", "wait"):
        for core in range(NC):
            low = pl.multiple_of((c ^ core) * half, half)
            for hop in range(NY):
                home = (y + hop) % NY
                piece = pieces[core * NY + hop]

                def body(k, carry):
                    m = order[home * RING + k]
                    copy = pltpu.make_async_copy(
                        piece.at[k], out.at[m, pl.ds(low, half)], sems.at[core, m]
                    )
                    getattr(copy, run)()
                    return carry

                lax.fori_loop(0, counts[home], body, 0)


def place(order, counts, where, pieces, count):
    _, half, columns = pieces[0].shape
    return pl.pallas_call(
        place_kernel,
        out_shape=jax.ShapeDtypeStruct((count, NC * half, columns), pieces[0].dtype),
        in_specs=[SMEM] * 3 + [ANY] * len(pieces),
        out_specs=HBM,
        scratch_shapes=[pltpu.SemaphoreType.DMA((NC, count))],
        name="place_blocks",
    )(order, counts, where, *pieces)


def spread(slots, owners, order, counts, where, blocks):
    own = select(owners, order, counts, where, blocks, slots)
    mine = [own, hop_y(own, -1), hop_y(own, 2), hop_y(own, 1)]
    other = [hop_core(piece) for piece in mine]
    return place(order, counts, where, mine + other, owners.shape[0])


def on_device(grads, momentum, owners):
    count = owners.shape[0]
    group = lax.axis_index("dp")
    me = lax.axis_index(AXES)
    where = jnp.stack([me // RING, me // SHARDS % NC]).astype(jnp.int32)
    packed = pack(owners, group[None].astype(jnp.int32), grads)
    rows = lax.all_to_all(packed, AXES, 0, 0, tiled=True, axis_index_groups=GROUPS_32)

    ids = jnp.arange(count, dtype=jnp.int32)
    homes = owners // RING
    before = (homes[:, None] == homes[None, :]) & (owners[None, :] < owners[:, None])
    slot = homes * RING + jnp.sum(before.astype(jnp.int32), axis=1)
    order = jnp.sum(
        jnp.where(slot[None, :] == jnp.arange(NY * RING, dtype=jnp.int32)[:, None], ids[None, :], 0), axis=1
    )
    counts = jnp.sum((homes[None, :] == jnp.arange(NY, dtype=jnp.int32)[:, None]).astype(jnp.int32), axis=1)
    owned = jnp.any(owners == me)[None].astype(jnp.int32)

    blocks, following = muon_step(owned, rows, momentum[0].T)
    blocks = lax.all_to_all(blocks, AXES, 0, 0, tiled=True, axis_index_groups=GROUPS_64)
    few = 34
    updates = lax.cond(
        jnp.max(counts) <= few,
        functools.partial(spread, few),
        functools.partial(spread, RING),
        owners,
        order,
        counts,
        where,
        blocks,
    )
    return (updates, following.T[None])


def solution(mesh):
    return jax.shard_map(
        on_device,
        mesh=mesh,
        in_specs=(P(None, "shard", None), P(AXES, None, None), P()),
        out_specs=(P(None, "shard", None), P(AXES, None, None)),
        check_vma=False,
    )
```

```python
import functools
import math

import jax
import jax.numpy as jnp
from jax import lax
from jax.experimental import pallas as pl
from jax.experimental.pallas import tpu as pltpu
from jax.sharding import PartitionSpec as P

DECAY = 0.95
LINEAR, CUBIC, QUINTIC = 3.4445, -4.775, 2.0315
EPS = 1e-07
ITERS = 2
AXES = ("dp", "shard")
NZ, NX, NC, NY = 8, 4, 2, 4
SHARDS = NZ * NX
RING = NC * SHARDS
NT = (((1,), (1,)), ((), ()))
NN = (((1,), (0,)), ((), ()))
ANY = pl.BlockSpec(memory_space=pl.ANY)
HBM = pl.BlockSpec(memory_space=pltpu.HBM)
SMEM = pl.BlockSpec(memory_space=pltpu.SMEM)
VMEM = pl.BlockSpec(memory_space=pltpu.VMEM)


def seat(z, x):
    pick = jnp.where if isinstance(z, jax.Array) else (lambda c, a, b: a if c else b)
    return pick(z < NZ // 2, 2 * z, 2 * NZ - 1 - 2 * z) + NZ * pick(x < NX // 2, 2 * x, 2 * NX - 1 - 2 * x)


SEATED = sorted(range(SHARDS), key=lambda s: seat(s // NX, s % NX))
GROUPS_32 = [[g * SHARDS + s for s in SEATED] for g in range(NY * NC)]
GROUPS_64 = [[y * RING + c * SHARDS + s for c in range(NC) for s in SEATED] for y in range(NY)]


def hop_y(array, step):
    count = NY * RING
    return lax.ppermute(array, AXES, [(d, (d + RING * step) % count) for d in range(count)])


def hop_core(array):
    return lax.ppermute(array, AXES, [(d, d ^ SHARDS) for d in range(NY * RING)])


def pack_kernel(owners, group, grads, out, sems):
    def copy(m):
        shard = owners[m] % SHARDS
        place = seat(shard // NX, shard % NX)
        return pltpu.make_async_copy(grads.at[m], out.at[place], sems.at[m])

    def start(m, carry):
        pl.when(owners[m] // SHARDS == group[0])(lambda: copy(m).start())
        return carry

    def wait(m, carry):
        pl.when(owners[m] // SHARDS == group[0])(lambda: copy(m).wait())
        return carry

    lax.fori_loop(0, owners.shape[0], start, 0)
    lax.fori_loop(0, owners.shape[0], wait, 0)


def pack(owners, group, grads):
    count, rows, columns = grads.shape
    return pl.pallas_call(
        pack_kernel,
        out_shape=jax.ShapeDtypeStruct((SHARDS, rows, columns), grads.dtype),
        in_specs=[SMEM, SMEM, HBM],
        out_specs=VMEM,
        scratch_shapes=[pltpu.SemaphoreType.DMA((count,))],
        name="pack_rows",
    )(owners, group, grads)


def dot(a, b, dims):
    return lax.dot_general(a, b, dims, preferred_element_type=jnp.float32)


def step_kernel(scale, owned_ref, rows_ref, mom_ref, out_ref, next_ref, blend, cur, gram, poly):
    rows = rows_ref.shape[1]
    half = rows // NC
    span = NX * rows
    owned = owned_ref[0] > 0
    total = jnp.zeros((8, span), jnp.float32)
    for z in range(NZ):
        cols = slice(z * span, (z + 1) * span)
        grad = jnp.concatenate([rows_ref[seat(z, x)] for x in range(NX)], axis=0)
        grad = jnp.where(owned, grad.T.astype(jnp.float32), 0.0)
        renewed = DECAY * mom_ref[:, cols].astype(jnp.float32) + grad
        next_ref[:, cols] = renewed.astype(jnp.bfloat16)
        mixed = grad + DECAY * renewed
        blend[:, cols] = mixed
        total = total + jnp.sum((mixed * mixed).reshape(-1, 8, span), axis=0)
    inverse = 1.0 / (jnp.sqrt(jnp.sum(total)) + EPS)
    cur[...] = (blend[...] * inverse).astype(jnp.bfloat16)
    for iteration in range(ITERS):
        x = cur[...]
        gram[...] = dot(x, x, NT).astype(jnp.bfloat16)
        g = gram[...]
        poly[...] = (CUBIC * g.astype(jnp.float32) + QUINTIC * dot(g, g, NN)).astype(jnp.bfloat16)
        if iteration + 1 < ITERS:
            cur[...] = (LINEAR * x.astype(jnp.float32) + dot(poly[...], x, NN)).astype(jnp.bfloat16)
            continue
        for z in range(NZ):
            xz = cur[:, z * span : (z + 1) * span]
            last = LINEAR * xz.astype(jnp.float32) + dot(poly[...], xz, NN)
            update = (scale * last).astype(jnp.bfloat16).T
            for x in range(NX):
                for c in range(NC):
                    low = x * rows + c * half
                    out_ref[c * SHARDS + seat(z, x)] = update[low : low + half]


def muon_step(owned, rows, momentum_t):
    columns, total_rows = momentum_t.shape
    scale = 0.2 * math.sqrt(max(columns, total_rows))
    square = pltpu.VMEM((columns, columns), jnp.bfloat16)
    return pl.pallas_call(
        functools.partial(step_kernel, scale),
        out_shape=(
            jax.ShapeDtypeStruct((RING, rows.shape[1] // NC, columns), jnp.bfloat16),
            jax.ShapeDtypeStruct(momentum_t.shape, jnp.bfloat16),
        ),
        in_specs=[SMEM, VMEM, VMEM],
        out_specs=(VMEM, VMEM),
        scratch_shapes=[
            pltpu.VMEM(momentum_t.shape, jnp.float32),
            pltpu.VMEM(momentum_t.shape, jnp.bfloat16),
            square,
            square,
        ],
        compiler_params=pltpu.CompilerParams(vmem_limit_bytes=48 * 2**20),
        name="newton_schulz",
    )(owned, rows, momentum_t)


def select_kernel(owners, order, counts, where, blocks, out):
    y = where[0]

    def body(k, carry):
        device = owners[order[y * RING + k]] % RING
        shard = device % SHARDS
        out[k] = blocks[device // SHARDS * SHARDS + seat(shard // NX, shard % NX)]
        return carry

    lax.fori_loop(0, counts[y], body, 0)


def select(owners, order, counts, where, blocks, slots):
    return pl.pallas_call(
        select_kernel,
        out_shape=jax.ShapeDtypeStruct((slots,) + blocks.shape[1:], blocks.dtype),
        in_specs=[SMEM] * 4 + [VMEM],
        out_specs=VMEM,
        name="select_blocks",
    )(owners, order, counts, where, blocks)


def place_kernel(origins, order, counts, where, *refs):
    pieces, out, sems = refs[: len(origins)], refs[len(origins)], refs[len(origins) + 1]
    y, c = where[0], where[1]
    half = out.shape[1] // NC
    for run in ("start", "wait"):
        for (core, hop, first), piece in zip(origins, pieces):
            low = pl.multiple_of((c ^ core) * half, half)
            home = (y + hop) % NY

            def body(k, carry):
                m = order[home * RING + k]
                copy = pltpu.make_async_copy(
                    piece.at[k - first], out.at[m, pl.ds(low, half)], sems.at[core, m]
                )
                getattr(copy, run)()
                return carry

            lax.fori_loop(first, jnp.minimum(counts[home], first + piece.shape[0]), body, 0)


def place(origins, order, counts, where, pieces, count):
    _, half, columns = pieces[0].shape
    return pl.pallas_call(
        functools.partial(place_kernel, origins),
        out_shape=jax.ShapeDtypeStruct((count, NC * half, columns), pieces[0].dtype),
        in_specs=[SMEM] * 3 + [VMEM] * len(pieces),
        out_specs=HBM,
        scratch_shapes=[pltpu.SemaphoreType.DMA((NC, count))],
        compiler_params=pltpu.CompilerParams(vmem_limit_bytes=48 * 2**20),
        name="place_blocks",
    )(order, counts, where, *pieces)


def spread(slots, owners, order, counts, where, blocks):
    own = select(owners, order, counts, where, blocks, slots)
    split = slots // 2
    below, above = hop_y(own, 1), hop_y(own, -1)
    mine = [own, above, below, hop_y(below[:split], 1), hop_y(above[split:], -1)]
    origins = [(0, 0, 0), (0, 1, 0), (0, 3, 0), (0, 2, 0), (0, 2, split)]
    pieces = mine + [hop_core(piece) for piece in mine]
    origins = origins + [(1, hop, first) for _, hop, first in origins]
    return place(origins, order, counts, where, pieces, owners.shape[0])


def on_device(grads, momentum, owners):
    count = owners.shape[0]
    group = lax.axis_index("dp")
    me = lax.axis_index(AXES)
    where = jnp.stack([me // RING, me // SHARDS % NC]).astype(jnp.int32)
    packed = pack(owners, group[None].astype(jnp.int32), grads)
    rows = lax.all_to_all(packed, AXES, 0, 0, tiled=True, axis_index_groups=GROUPS_32)

    ids = jnp.arange(count, dtype=jnp.int32)
    homes = owners // RING
    before = (homes[:, None] == homes[None, :]) & (owners[None, :] < owners[:, None])
    slot = homes * RING + jnp.sum(before.astype(jnp.int32), axis=1)
    order = jnp.sum(
        jnp.where(slot[None, :] == jnp.arange(NY * RING, dtype=jnp.int32)[:, None], ids[None, :], 0), axis=1
    )
    counts = jnp.sum((homes[None, :] == jnp.arange(NY, dtype=jnp.int32)[:, None]).astype(jnp.int32), axis=1)
    owned = jnp.any(owners == me)[None].astype(jnp.int32)

    blocks, following = muon_step(owned, rows, momentum[0].T)
    blocks = lax.all_to_all(blocks, AXES, 0, 0, tiled=True, axis_index_groups=GROUPS_64)
    sizes = (28, 30, 32, 34, 36, RING)
    updates = lax.switch(
        jnp.sum((jnp.max(counts) > jnp.array(sizes[:-1])).astype(jnp.int32)),
        [functools.partial(spread, slots) for slots in sizes],
        owners,
        order,
        counts,
        where,
        blocks,
    )
    return (updates, following.T[None])


def solution(mesh):
    return jax.shard_map(
        on_device,
        mesh=mesh,
        in_specs=(P(None, "shard", None), P(AXES, None, None), P()),
        out_specs=(P(None, "shard", None), P(AXES, None, None)),
        check_vma=False,
    )
```

```python
import functools
import math

import jax
import jax.numpy as jnp
from jax import lax
from jax.experimental import pallas as pl
from jax.experimental.pallas import tpu as pltpu
from jax.sharding import PartitionSpec as P

DECAY = 0.95
LINEAR, CUBIC, QUINTIC = 3.4445, -4.775, 2.0315
EPS = 1e-07
ITERS = 2
AXES = ("dp", "shard")
NZ, NX, NC, NY = 8, 4, 2, 4
SHARDS = NZ * NX
RING = NC * SHARDS
NT = (((1,), (1,)), ((), ()))
NN = (((1,), (0,)), ((), ()))
ANY = pl.BlockSpec(memory_space=pl.ANY)
HBM = pl.BlockSpec(memory_space=pltpu.HBM)
SMEM = pl.BlockSpec(memory_space=pltpu.SMEM)
VMEM = pl.BlockSpec(memory_space=pltpu.VMEM)


def seat(z, x):
    pick = jnp.where if isinstance(z, jax.Array) else (lambda c, a, b: a if c else b)
    return pick(z < NZ // 2, 2 * z, 2 * NZ - 1 - 2 * z) + NZ * pick(x < NX // 2, 2 * x, 2 * NX - 1 - 2 * x)


SEATED = sorted(range(SHARDS), key=lambda s: seat(s // NX, s % NX))
GROUPS_32 = [[g * SHARDS + s for s in SEATED] for g in range(NY * NC)]
GROUPS_64 = [[y * RING + c * SHARDS + s for c in range(NC) for s in SEATED] for y in range(NY)]


def hop_y(array, step):
    count = NY * RING
    return lax.ppermute(array, AXES, [(d, (d + RING * step) % count) for d in range(count)])


def hop_core(array):
    return lax.ppermute(array, AXES, [(d, d ^ SHARDS) for d in range(NY * RING)])


def pack_kernel(owners, group, grads, out, sems):
    count, unroll = owners.shape[0], 8

    def copy(m, place, k):
        return pltpu.make_async_copy(grads.at[m], out.at[place], sems.at[k])

    def look(m, found):
        owner = owners[m]
        mine = (owner >> 5) == group[0]

        @pl.when(mine)
        def _():
            copy(m, seat((owner >> 2) & (NZ - 1), owner & (NX - 1)), found).start()

        return found + mine.astype(jnp.int32)

    def look_many(i, found):
        for j in range(unroll):
            found = look(i * unroll + j, found)
        return found

    found = lax.fori_loop(0, count // unroll, look_many, jnp.int32(0))
    for m in range(count // unroll * unroll, count):
        found = look(m, found)

    def wait(k, carry):
        copy(0, 0, k).wait()
        return carry

    lax.fori_loop(0, found, wait, 0)


def pack(owners, group, grads):
    count, rows, columns = grads.shape
    return pl.pallas_call(
        pack_kernel,
        out_shape=jax.ShapeDtypeStruct((SHARDS, rows, columns), grads.dtype),
        in_specs=[SMEM, SMEM, HBM],
        out_specs=VMEM,
        scratch_shapes=[pltpu.SemaphoreType.DMA((count,))],
        name="pack_rows",
    )(owners, group, grads)


def dot(a, b, dims):
    return lax.dot_general(a, b, dims, preferred_element_type=jnp.float32)


def step_kernel(scale, owned_ref, rows_ref, mom_ref, out_ref, next_ref, blend, cur, gram, poly):
    rows = rows_ref.shape[1]
    half = rows // NC
    span = NX * rows
    owned = owned_ref[0] > 0
    total = jnp.zeros((8, span), jnp.float32)
    for z in range(NZ):
        cols = slice(z * span, (z + 1) * span)
        grad = jnp.concatenate([rows_ref[seat(z, x)] for x in range(NX)], axis=0)
        grad = jnp.where(owned, grad.T.astype(jnp.float32), 0.0)
        renewed = DECAY * mom_ref[:, cols].astype(jnp.float32) + grad
        next_ref[:, cols] = renewed.astype(jnp.bfloat16)
        mixed = grad + DECAY * renewed
        blend[:, cols] = mixed
        total = total + jnp.sum((mixed * mixed).reshape(-1, 8, span), axis=0)
    inverse = 1.0 / (jnp.sqrt(jnp.sum(total)) + EPS)
    cur[...] = (blend[...] * inverse).astype(jnp.bfloat16)
    for iteration in range(ITERS):
        x = cur[...]
        gram[...] = dot(x, x, NT).astype(jnp.bfloat16)
        g = gram[...]
        poly[...] = (CUBIC * g.astype(jnp.float32) + QUINTIC * dot(g, g, NN)).astype(jnp.bfloat16)
        if iteration + 1 < ITERS:
            cur[...] = (LINEAR * x.astype(jnp.float32) + dot(poly[...], x, NN)).astype(jnp.bfloat16)
            continue
        for z in range(NZ):
            xz = cur[:, z * span : (z + 1) * span]
            last = LINEAR * xz.astype(jnp.float32) + dot(poly[...], xz, NN)
            update = (scale * last).astype(jnp.bfloat16).T
            for x in range(NX):
                for c in range(NC):
                    low = x * rows + c * half
                    out_ref[c * SHARDS + seat(z, x)] = update[low : low + half]


def muon_step(owned, rows, momentum_t):
    columns, total_rows = momentum_t.shape
    scale = 0.2 * math.sqrt(max(columns, total_rows))
    square = pltpu.VMEM((columns, columns), jnp.bfloat16)
    return pl.pallas_call(
        functools.partial(step_kernel, scale),
        out_shape=(
            jax.ShapeDtypeStruct((RING, rows.shape[1] // NC, columns), jnp.bfloat16),
            jax.ShapeDtypeStruct(momentum_t.shape, jnp.bfloat16),
        ),
        in_specs=[SMEM, VMEM, VMEM],
        out_specs=(VMEM, VMEM),
        scratch_shapes=[
            pltpu.VMEM(momentum_t.shape, jnp.float32),
            pltpu.VMEM(momentum_t.shape, jnp.bfloat16),
            square,
            square,
        ],
        compiler_params=pltpu.CompilerParams(vmem_limit_bytes=48 * 2**20),
        name="newton_schulz",
    )(owned, rows, momentum_t)


def select_kernel(seats, order, counts, where, blocks, out):
    y = where[0]

    def body(k, carry):
        out[k] = blocks[seats[order[y * RING + k]]]
        return carry

    lax.fori_loop(0, counts[y], body, 0)


def select(seats, order, counts, where, blocks, slots):
    return pl.pallas_call(
        select_kernel,
        out_shape=jax.ShapeDtypeStruct((slots,) + blocks.shape[1:], blocks.dtype),
        in_specs=[SMEM] * 4 + [VMEM],
        out_specs=VMEM,
        name="select_blocks",
    )(seats, order, counts, where, blocks)


def place_kernel(origins, order, counts, where, *refs):
    pieces, out, sems = refs[: len(origins)], refs[-2], refs[-1]
    y, c = where[0], where[1]
    half = out.shape[1] // NC
    for run in ("start", "wait"):
        for (core, hop, first), piece in zip(origins, pieces):
            low = pl.multiple_of((c ^ core) * half, half)
            home = (y + hop) & (NY - 1)

            def body(k, carry):
                m = order[home * RING + k]
                copy = pltpu.make_async_copy(
                    piece.at[k - first], out.at[m, pl.ds(low, half)], sems.at[core, m]
                )
                getattr(copy, run)()
                return carry

            lax.fori_loop(first, jnp.minimum(counts[home], first + piece.shape[0]), body, 0)


def place(origins, order, counts, where, pieces, count, base=None):
    _, half, columns = pieces[0].shape
    bases = [] if base is None else [base]
    return pl.pallas_call(
        functools.partial(place_kernel, origins),
        out_shape=jax.ShapeDtypeStruct((count, NC * half, columns), pieces[0].dtype),
        in_specs=[SMEM] * 3 + [VMEM] * len(pieces) + [HBM] * len(bases),
        out_specs=HBM,
        input_output_aliases={3 + len(pieces): 0} if bases else {},
        scratch_shapes=[pltpu.SemaphoreType.DMA((NC, count))],
        compiler_params=pltpu.CompilerParams(vmem_limit_bytes=48 * 2**20),
        name="place_blocks",
    )(order, counts, where, *pieces, *bases)


def spread(slots, seats, order, counts, where, blocks):
    count = seats.shape[0]
    own = select(seats, order, counts, where, blocks, slots)
    split = slots // 2
    below, above = hop_y(own, 1), hop_y(own, -1)
    opposite = (hop_y(below[:split], 1), hop_y(above[split:], -1))
    near = [own, above, below]
    near += [hop_core(piece) for piece in near]
    origins = [(core, hop, 0) for core in range(NC) for hop in (0, 1, 3)]
    updates = place(origins, order, counts, where, near, count)
    updates, low, high = lax.optimization_barrier((updates,) + opposite)
    far = [low, high, hop_core(low), hop_core(high)]
    origins = [(core, 2, first) for core in range(NC) for first in (0, split)]
    return place(origins, order, counts, where, far, count, updates)


def on_device(grads, momentum, owners):
    count = owners.shape[0]
    group = lax.axis_index("dp")
    me = lax.axis_index(AXES)
    where = jnp.stack([me // RING, me // SHARDS % NC]).astype(jnp.int32)
    packed = pack(owners, group[None].astype(jnp.int32), grads)
    rows = lax.all_to_all(packed, AXES, 0, 0, tiled=True, axis_index_groups=GROUPS_32)

    ids = jnp.arange(count, dtype=jnp.int32)
    homes = owners // RING
    seats = (owners & SHARDS) + seat((owners >> 2) & (NZ - 1), owners & (NX - 1))
    before = (homes[:, None] == homes[None, :]) & (owners[None, :] < owners[:, None])
    slot = homes * RING + jnp.sum(before.astype(jnp.int32), axis=1)
    order = jnp.sum(
        jnp.where(slot[None, :] == jnp.arange(NY * RING, dtype=jnp.int32)[:, None], ids[None, :], 0), axis=1
    )
    counts = jnp.sum((homes[None, :] == jnp.arange(NY, dtype=jnp.int32)[:, None]).astype(jnp.int32), axis=1)
    owned = jnp.any(owners == me)[None].astype(jnp.int32)

    blocks, following = muon_step(owned, rows, momentum[0].T)
    blocks = lax.all_to_all(blocks, AXES, 0, 0, tiled=True, axis_index_groups=GROUPS_64)
    few = 34
    updates = lax.cond(
        jnp.max(counts) <= few,
        functools.partial(spread, few),
        functools.partial(spread, RING),
        seats,
        order,
        counts,
        where,
        blocks,
    )
    return (updates, following.T[None])


def solution(mesh):
    return jax.shard_map(
        on_device,
        mesh=mesh,
        in_specs=(P(None, "shard", None), P(AXES, None, None), P()),
        out_specs=(P(None, "shard", None), P(AXES, None, None)),
        check_vma=False,
    )
```

```python
import functools
import math

import jax
import jax.numpy as jnp
from jax import lax
from jax.experimental import pallas as pl
from jax.experimental.pallas import tpu as pltpu
from jax.sharding import PartitionSpec as P

DECAY = 0.95
LINEAR, CUBIC, QUINTIC = 3.4445, -4.775, 2.0315
EPS = 1e-07
ITERS = 2
AXES = ("dp", "shard")
NZ, NX, NC, NY = 8, 4, 2, 4
SHARDS = NZ * NX
RING = NC * SHARDS
NT = (((1,), (1,)), ((), ()))
NN = (((1,), (0,)), ((), ()))
ANY = pl.BlockSpec(memory_space=pl.ANY)
HBM = pl.BlockSpec(memory_space=pltpu.HBM)
SMEM = pl.BlockSpec(memory_space=pltpu.SMEM)
VMEM = pl.BlockSpec(memory_space=pltpu.VMEM)


def seat(z, x):
    pick = jnp.where if isinstance(z, jax.Array) else (lambda c, a, b: a if c else b)
    return pick(z < NZ // 2, 2 * z, 2 * NZ - 1 - 2 * z) + NZ * pick(x < NX // 2, 2 * x, 2 * NX - 1 - 2 * x)


SEATED = sorted(range(SHARDS), key=lambda s: seat(s // NX, s % NX))
GROUPS_32 = [[g * SHARDS + s for s in SEATED] for g in range(NY * NC)]
GROUPS_64 = [[y * RING + c * SHARDS + s for c in range(NC) for s in SEATED] for y in range(NY)]


def hop_y(array, step):
    count = NY * RING
    return lax.ppermute(array, AXES, [(d, (d + RING * step) % count) for d in range(count)])


def hop_core(array):
    return lax.ppermute(array, AXES, [(d, d ^ SHARDS) for d in range(NY * RING)])


def pack_kernel(owners, group, grads, out, sems):
    count, unroll = owners.shape[0], 8

    def copy(m, place, k):
        return pltpu.make_async_copy(grads.at[m], out.at[place], sems.at[k])

    def look(m, found):
        owner = owners[m]
        mine = (owner >> 5) == group[0]

        @pl.when(mine)
        def _():
            copy(m, seat((owner >> 2) & (NZ - 1), owner & (NX - 1)), found).start()

        return found + mine.astype(jnp.int32)

    def look_many(i, found):
        for j in range(unroll):
            found = look(i * unroll + j, found)
        return found

    found = lax.fori_loop(0, count // unroll, look_many, jnp.int32(0))
    for m in range(count // unroll * unroll, count):
        found = look(m, found)

    def wait(k, carry):
        copy(0, 0, k).wait()
        return carry

    lax.fori_loop(0, found, wait, 0)


def pack(owners, group, grads):
    count, rows, columns = grads.shape
    return pl.pallas_call(
        pack_kernel,
        out_shape=jax.ShapeDtypeStruct((SHARDS, rows, columns), grads.dtype),
        in_specs=[SMEM, SMEM, HBM],
        out_specs=VMEM,
        scratch_shapes=[pltpu.SemaphoreType.DMA((count,))],
        name="pack_rows",
    )(owners, group, grads)


def dot(a, b, dims):
    return lax.dot_general(a, b, dims, preferred_element_type=jnp.float32)


def step_kernel(scale, owned_ref, rows_ref, mom_ref, out_ref, next_ref, blend, cur, gram, poly):
    rows = rows_ref.shape[1]
    half = rows // NC
    span = NX * rows
    owned = owned_ref[0] > 0
    total = jnp.zeros((8, span), jnp.float32)
    for z in range(NZ):
        cols = slice(z * span, (z + 1) * span)
        grad = jnp.concatenate([rows_ref[seat(z, x)] for x in range(NX)], axis=0)
        grad = jnp.where(owned, grad.T.astype(jnp.float32), 0.0)
        renewed = DECAY * mom_ref[:, cols].astype(jnp.float32) + grad
        next_ref[:, cols] = renewed.astype(jnp.bfloat16)
        mixed = grad + DECAY * renewed
        blend[:, cols] = mixed
        total = total + jnp.sum((mixed * mixed).reshape(-1, 8, span), axis=0)
    inverse = 1.0 / (jnp.sqrt(jnp.sum(total)) + EPS)
    cur[...] = (blend[...] * inverse).astype(jnp.bfloat16)
    for iteration in range(ITERS):
        x = cur[...]
        gram[...] = dot(x, x, NT).astype(jnp.bfloat16)
        g = gram[...]
        poly[...] = (CUBIC * g.astype(jnp.float32) + QUINTIC * dot(g, g, NN)).astype(jnp.bfloat16)
        if iteration + 1 < ITERS:
            cur[...] = (LINEAR * x.astype(jnp.float32) + dot(poly[...], x, NN)).astype(jnp.bfloat16)
            continue
        for z in range(NZ):
            xz = cur[:, z * span : (z + 1) * span]
            last = LINEAR * xz.astype(jnp.float32) + dot(poly[...], xz, NN)
            update = (scale * last).astype(jnp.bfloat16).T
            for x in range(NX):
                for c in range(NC):
                    low = x * rows + c * half
                    out_ref[c * SHARDS + seat(z, x)] = update[low : low + half]


def muon_step(owned, rows, momentum_t):
    columns, total_rows = momentum_t.shape
    scale = 0.2 * math.sqrt(max(columns, total_rows))
    square = pltpu.VMEM((columns, columns), jnp.bfloat16)
    return pl.pallas_call(
        functools.partial(step_kernel, scale),
        out_shape=(
            jax.ShapeDtypeStruct((RING, rows.shape[1] // NC, columns), jnp.bfloat16),
            jax.ShapeDtypeStruct(momentum_t.shape, jnp.bfloat16),
        ),
        in_specs=[SMEM, VMEM, VMEM],
        out_specs=(VMEM, VMEM),
        scratch_shapes=[
            pltpu.VMEM(momentum_t.shape, jnp.float32),
            pltpu.VMEM(momentum_t.shape, jnp.bfloat16),
            square,
            square,
        ],
        compiler_params=pltpu.CompilerParams(vmem_limit_bytes=48 * 2**20),
        name="newton_schulz",
    )(owned, rows, momentum_t)


def select_kernel(seats, order, counts, where, blocks, low, high):
    y = where[0]
    split = low.shape[0]
    for out, first, last in ((low, 0, jnp.minimum(counts[y], split)), (high, split, counts[y])):

        def body(k, carry):
            out[k - first] = blocks[seats[order[y * RING + k]]]
            return carry

        lax.fori_loop(first, last, body, 0)


def select(seats, order, counts, where, blocks, slots):
    out = jax.ShapeDtypeStruct((slots // 2,) + blocks.shape[1:], blocks.dtype)
    return pl.pallas_call(
        select_kernel,
        out_shape=(out, out),
        in_specs=[SMEM] * 4 + [VMEM],
        out_specs=(VMEM, VMEM),
        name="select_blocks",
    )(seats, order, counts, where, blocks)


def place_kernel(origins, order, counts, where, *refs):
    pieces, out, sems = refs[: len(origins)], refs[-2], refs[-1]
    y, c = where[0], where[1]
    half = out.shape[1] // NC
    for run in ("start", "wait"):
        for (core, hop, first), piece in zip(origins, pieces):
            low = pl.multiple_of((c ^ core) * half, half)
            home = (y + hop) & (NY - 1)

            def body(k, carry):
                m = order[home * RING + k]
                copy = pltpu.make_async_copy(
                    piece.at[k - first], out.at[m, pl.ds(low, half)], sems.at[core, m]
                )
                getattr(copy, run)()
                return carry

            lax.fori_loop(first, jnp.minimum(counts[home], first + piece.shape[0]), body, 0)


def place(origins, order, counts, where, pieces, count, base=None):
    _, half, columns = pieces[0].shape
    bases = [] if base is None else [base]
    return pl.pallas_call(
        functools.partial(place_kernel, origins),
        out_shape=jax.ShapeDtypeStruct((count, NC * half, columns), pieces[0].dtype),
        in_specs=[SMEM] * 3 + [VMEM] * len(pieces) + [HBM] * len(bases),
        out_specs=HBM,
        input_output_aliases={3 + len(pieces): 0} if bases else {},
        scratch_shapes=[pltpu.SemaphoreType.DMA((NC, count))],
        compiler_params=pltpu.CompilerParams(vmem_limit_bytes=48 * 2**20),
        name="place_blocks",
    )(order, counts, where, *pieces, *bases)


def spread(slots, seats, order, counts, where, blocks):
    count = seats.shape[0]
    split = slots // 2
    low, high = select(seats, order, counts, where, blocks, slots)
    below_low, above_high = hop_y(low, 1), hop_y(high, -1)
    below_high, above_low = hop_y(high, 1), hop_y(low, -1)
    far = [hop_y(below_low, 1), hop_y(above_high, -1)]
    near = [low, high, above_low, above_high, below_low, below_high]
    near += [hop_core(piece) for piece in near]
    origins = [(core, hop, first) for core in range(NC) for hop in (0, 1, 3) for first in (0, split)]
    updates = place(origins, order, counts, where, near, count)
    updates, *far = lax.optimization_barrier([updates] + far)
    far += [hop_core(piece) for piece in far]
    origins = [(core, 2, first) for core in range(NC) for first in (0, split)]
    return place(origins, order, counts, where, far, count, updates)


def on_device(grads, momentum, owners):
    count = owners.shape[0]
    group = lax.axis_index("dp")
    me = lax.axis_index(AXES)
    where = jnp.stack([me // RING, me // SHARDS % NC]).astype(jnp.int32)
    packed = pack(owners, group[None].astype(jnp.int32), grads)
    rows = lax.all_to_all(packed, AXES, 0, 0, tiled=True, axis_index_groups=GROUPS_32)

    ids = jnp.arange(count, dtype=jnp.int32)
    homes = owners // RING
    seats = (owners & SHARDS) + seat((owners >> 2) & (NZ - 1), owners & (NX - 1))
    before = (homes[:, None] == homes[None, :]) & (owners[None, :] < owners[:, None])
    slot = homes * RING + jnp.sum(before.astype(jnp.int32), axis=1)
    order = jnp.sum(
        jnp.where(slot[None, :] == jnp.arange(NY * RING, dtype=jnp.int32)[:, None], ids[None, :], 0), axis=1
    )
    counts = jnp.sum((homes[None, :] == jnp.arange(NY, dtype=jnp.int32)[:, None]).astype(jnp.int32), axis=1)
    owned = jnp.any(owners == me)[None].astype(jnp.int32)

    blocks, following = muon_step(owned, rows, momentum[0].T)
    blocks = lax.all_to_all(blocks, AXES, 0, 0, tiled=True, axis_index_groups=GROUPS_64)
    few = 34
    updates = lax.cond(
        jnp.max(counts) <= few,
        functools.partial(spread, few),
        functools.partial(spread, RING),
        seats,
        order,
        counts,
        where,
        blocks,
    )
    return (updates, following.T[None])


def solution(mesh):
    return jax.shard_map(
        on_device,
        mesh=mesh,
        in_specs=(P(None, "shard", None), P(AXES, None, None), P()),
        out_specs=(P(None, "shard", None), P(AXES, None, None)),
        check_vma=False,
    )
```

```python
import functools
import math

import jax
import jax.numpy as jnp
from jax import lax
from jax.experimental import pallas as pl
from jax.experimental.pallas import tpu as pltpu
from jax.sharding import PartitionSpec as P

DECAY = 0.95
LINEAR, CUBIC, QUINTIC = 3.4445, -4.775, 2.0315
EPS = 1e-07
ITERS = 2
AXES = ("dp", "shard")
NZ, NX, NC, NY = 8, 4, 2, 4
SHARDS = NZ * NX
RING = NC * SHARDS
NT = (((1,), (1,)), ((), ()))
NN = (((1,), (0,)), ((), ()))
ANY = pl.BlockSpec(memory_space=pl.ANY)
HBM = pl.BlockSpec(memory_space=pltpu.HBM)
SMEM = pl.BlockSpec(memory_space=pltpu.SMEM)
VMEM = pl.BlockSpec(memory_space=pltpu.VMEM)


def seat(z, x):
    pick = jnp.where if isinstance(z, jax.Array) else (lambda c, a, b: a if c else b)
    return pick(z < NZ // 2, 2 * z, 2 * NZ - 1 - 2 * z) + NZ * pick(x < NX // 2, 2 * x, 2 * NX - 1 - 2 * x)


SEATED = sorted(range(SHARDS), key=lambda s: seat(s // NX, s % NX))
GROUPS_32 = [[g * SHARDS + s for s in SEATED] for g in range(NY * NC)]
GROUPS_64 = [[y * RING + c * SHARDS + s for c in range(NC) for s in SEATED] for y in range(NY)]


def hop_y(array, step):
    count = NY * RING
    return lax.ppermute(array, AXES, [(d, (d + RING * step) % count) for d in range(count)])


def hop_core(array):
    return lax.ppermute(array, AXES, [(d, d ^ SHARDS) for d in range(NY * RING)])


def pack_kernel(owners, group, grads, out, sems):
    count, unroll = owners.shape[0], 8

    def copy(m, place, k):
        return pltpu.make_async_copy(grads.at[m], out.at[place], sems.at[k])

    def look(m, found):
        owner = owners[m]
        mine = (owner >> 5) == group[0]

        @pl.when(mine)
        def _():
            copy(m, seat((owner >> 2) & (NZ - 1), owner & (NX - 1)), found).start()

        return found + mine.astype(jnp.int32)

    def look_many(i, found):
        for j in range(unroll):
            found = look(i * unroll + j, found)
        return found

    found = lax.fori_loop(0, count // unroll, look_many, jnp.int32(0))
    for m in range(count // unroll * unroll, count):
        found = look(m, found)

    def wait(k, carry):
        copy(0, 0, k).wait()
        return carry

    lax.fori_loop(0, found, wait, 0)


def pack(owners, group, grads):
    count, rows, columns = grads.shape
    return pl.pallas_call(
        pack_kernel,
        out_shape=jax.ShapeDtypeStruct((SHARDS, rows, columns), grads.dtype),
        in_specs=[SMEM, SMEM, HBM],
        out_specs=VMEM,
        scratch_shapes=[pltpu.SemaphoreType.DMA((count,))],
        name="pack_rows",
    )(owners, group, grads)


def dot(a, b, dims):
    return lax.dot_general(a, b, dims, preferred_element_type=jnp.float32)


def step_kernel(scale, owned_ref, rows_ref, mom_ref, out_ref, next_ref, blend, cur, gram, poly):
    rows = rows_ref.shape[1]
    half = rows // NC
    span = NX * rows
    owned = owned_ref[0] > 0
    total = jnp.zeros((8, span), jnp.float32)
    for z in range(NZ):
        cols = slice(z * span, (z + 1) * span)
        grad = jnp.concatenate([rows_ref[seat(z, x)] for x in range(NX)], axis=0)
        grad = jnp.where(owned, grad.T.astype(jnp.float32), 0.0)
        renewed = DECAY * mom_ref[:, cols].astype(jnp.float32) + grad
        next_ref[:, cols] = renewed.astype(jnp.bfloat16)
        mixed = grad + DECAY * renewed
        blend[:, cols] = mixed
        total = total + jnp.sum((mixed * mixed).reshape(-1, 8, span), axis=0)
    inverse = 1.0 / (jnp.sqrt(jnp.sum(total)) + EPS)
    cur[...] = (blend[...] * inverse).astype(jnp.bfloat16)
    columns, total_rows = cur.shape
    cuts = [(low, min(low + 256, columns)) for low in range(0, columns, 256)]
    wide = 2 * span
    for iteration in range(ITERS):
        for low, high in cuts:
            block = dot(cur[:high], cur[low:high], NT).astype(jnp.bfloat16)
            gram[:high, low:high] = block
            if low:
                gram[low:high, :low] = block[:low].T
        for low, high in cuts:
            square = dot(gram[:high], gram[:, low:high], NN)
            block = (CUBIC * gram[:high, low:high].astype(jnp.float32) + QUINTIC * square).astype(jnp.bfloat16)
            poly[:high, low:high] = block
            if low:
                poly[low:high, :low] = block[:low].T
        factor = poly[...]
        if iteration + 1 < ITERS:
            x = cur[...]
            cur[...] = (LINEAR * x.astype(jnp.float32) + dot(factor, x, NN)).astype(jnp.bfloat16)
            continue
        for left in range(0, total_rows, wide):
            x = cur[:, left : left + wide]
            last = (scale * LINEAR) * x.astype(jnp.float32) + scale * dot(factor, x, NN)
            last = last.astype(jnp.bfloat16)
            for z in range(left // span, (left + wide) // span):
                update = last[:, z * span - left : (z + 1) * span - left].T
                for x in range(NX):
                    for c in range(NC):
                        low = x * rows + c * half
                        out_ref[c * SHARDS + seat(z, x)] = update[low : low + half]


def muon_step(owned, rows, momentum_t):
    columns, total_rows = momentum_t.shape
    scale = 0.2 * math.sqrt(max(columns, total_rows))
    square = pltpu.VMEM((columns, columns), jnp.bfloat16)
    return pl.pallas_call(
        functools.partial(step_kernel, scale),
        out_shape=(
            jax.ShapeDtypeStruct((RING, rows.shape[1] // NC, columns), jnp.bfloat16),
            jax.ShapeDtypeStruct(momentum_t.shape, jnp.bfloat16),
        ),
        in_specs=[SMEM, VMEM, VMEM],
        out_specs=(VMEM, VMEM),
        scratch_shapes=[
            pltpu.VMEM(momentum_t.shape, jnp.float32),
            pltpu.VMEM(momentum_t.shape, jnp.bfloat16),
            square,
            square,
        ],
        compiler_params=pltpu.CompilerParams(vmem_limit_bytes=48 * 2**20),
        name="newton_schulz",
    )(owned, rows, momentum_t)


def select_kernel(seats, order, counts, where, blocks, low, high):
    y = where[0]
    split = low.shape[0]
    for out, first, last in ((low, 0, jnp.minimum(counts[y], split)), (high, split, counts[y])):

        def body(k, carry):
            out[k - first] = blocks[seats[order[y * RING + k]]]
            return carry

        lax.fori_loop(first, last, body, 0)


def select(seats, order, counts, where, blocks, slots):
    out = jax.ShapeDtypeStruct((slots // 2,) + blocks.shape[1:], blocks.dtype)
    return pl.pallas_call(
        select_kernel,
        out_shape=(out, out),
        in_specs=[SMEM] * 4 + [VMEM],
        out_specs=(VMEM, VMEM),
        name="select_blocks",
    )(seats, order, counts, where, blocks)


def place_kernel(origins, order, counts, where, *refs):
    pieces, out, sems = refs[: len(origins)], refs[-2], refs[-1]
    y, c = where[0], where[1]
    half = out.shape[1] // NC
    for run in ("start", "wait"):
        for (core, hop, first), piece in zip(origins, pieces):
            low = pl.multiple_of((c ^ core) * half, half)
            home = (y + hop) & (NY - 1)

            def body(k, carry):
                m = order[home * RING + k]
                copy = pltpu.make_async_copy(
                    piece.at[k - first], out.at[m, pl.ds(low, half)], sems.at[core, m]
                )
                getattr(copy, run)()
                return carry

            lax.fori_loop(first, jnp.minimum(counts[home], first + piece.shape[0]), body, 0)


def place(origins, order, counts, where, pieces, count, base=None):
    _, half, columns = pieces[0].shape
    bases = [] if base is None else [base]
    return pl.pallas_call(
        functools.partial(place_kernel, origins),
        out_shape=jax.ShapeDtypeStruct((count, NC * half, columns), pieces[0].dtype),
        in_specs=[SMEM] * 3 + [VMEM] * len(pieces) + [HBM] * len(bases),
        out_specs=HBM,
        input_output_aliases={3 + len(pieces): 0} if bases else {},
        scratch_shapes=[pltpu.SemaphoreType.DMA((NC, count))],
        compiler_params=pltpu.CompilerParams(vmem_limit_bytes=48 * 2**20),
        name="place_blocks",
    )(order, counts, where, *pieces, *bases)


def spread(slots, seats, order, counts, where, blocks):
    count = seats.shape[0]
    split = slots // 2
    low, high = select(seats, order, counts, where, blocks, slots)
    below_low, above_high = hop_y(low, 1), hop_y(high, -1)
    below_high, above_low = hop_y(high, 1), hop_y(low, -1)
    far = [hop_y(below_low, 1), hop_y(above_high, -1)]
    early = lax.optimization_barrier([low, high, below_low, above_high])
    early += [hop_core(piece) for piece in early]
    origins = [(core, *origin) for core in range(NC) for origin in ((0, 0), (0, split), (3, 0), (1, split))]
    updates = place(origins, order, counts, where, early, count)
    late = lax.optimization_barrier([below_high, above_low] + far)
    late += [hop_core(piece) for piece in late]
    origins = [(core, *origin) for core in range(NC) for origin in ((3, split), (1, 0), (2, 0), (2, split))]
    return place(origins, order, counts, where, late, count, updates)


def on_device(grads, momentum, owners):
    count = owners.shape[0]
    group = lax.axis_index("dp")
    me = lax.axis_index(AXES)
    where = jnp.stack([me // RING, me // SHARDS % NC]).astype(jnp.int32)
    packed = pack(owners, group[None].astype(jnp.int32), grads)
    rows = lax.all_to_all(packed, AXES, 0, 0, tiled=True, axis_index_groups=GROUPS_32)

    ids = jnp.arange(count, dtype=jnp.int32)
    homes = owners // RING
    seats = (owners & SHARDS) + seat((owners >> 2) & (NZ - 1), owners & (NX - 1))
    before = (homes[:, None] == homes[None, :]) & (owners[None, :] < owners[:, None])
    slot = homes * RING + jnp.sum(before.astype(jnp.int32), axis=1)
    order = jnp.sum(
        jnp.where(slot[None, :] == jnp.arange(NY * RING, dtype=jnp.int32)[:, None], ids[None, :], 0), axis=1
    )
    counts = jnp.sum((homes[None, :] == jnp.arange(NY, dtype=jnp.int32)[:, None]).astype(jnp.int32), axis=1)
    owned = jnp.any(owners == me)[None].astype(jnp.int32)

    blocks, following = muon_step(owned, rows, momentum[0].T)
    blocks = lax.all_to_all(blocks, AXES, 0, 0, tiled=True, axis_index_groups=GROUPS_64)
    few = 34
    updates = lax.cond(
        jnp.max(counts) <= few,
        functools.partial(spread, few),
        functools.partial(spread, RING),
        seats,
        order,
        counts,
        where,
        blocks,
    )
    return (updates, following.T[None])


def solution(mesh):
    return jax.shard_map(
        on_device,
        mesh=mesh,
        in_specs=(P(None, "shard", None), P(AXES, None, None), P()),
        out_specs=(P(None, "shard", None), P(AXES, None, None)),
        check_vma=False,
    )
```

```python
import functools
import math

import jax
import jax.numpy as jnp
from jax import lax
from jax.experimental import pallas as pl
from jax.experimental.pallas import tpu as pltpu
from jax.sharding import PartitionSpec as P

DECAY = 0.95
LINEAR, CUBIC, QUINTIC = 3.4445, -4.775, 2.0315
EPS = 1e-07
ITERS = 2
AXES = ("dp", "shard")
NZ, NX, NC, NY = 8, 4, 2, 4
SHARDS = NZ * NX
RING = NC * SHARDS
NT = (((1,), (1,)), ((), ()))
NN = (((1,), (0,)), ((), ()))
ANY = pl.BlockSpec(memory_space=pl.ANY)
HBM = pl.BlockSpec(memory_space=pltpu.HBM)
SMEM = pl.BlockSpec(memory_space=pltpu.SMEM)
VMEM = pl.BlockSpec(memory_space=pltpu.VMEM)


def seat(z, x):
    pick = jnp.where if isinstance(z, jax.Array) else (lambda c, a, b: a if c else b)
    return pick(z < NZ // 2, 2 * z, 2 * NZ - 1 - 2 * z) + NZ * pick(x < NX // 2, 2 * x, 2 * NX - 1 - 2 * x)


SEATED = sorted(range(SHARDS), key=lambda s: seat(s // NX, s % NX))
GROUPS_32 = [[g * SHARDS + s for s in SEATED] for g in range(NY * NC)]
GROUPS_64 = [[y * RING + c * SHARDS + s for c in range(NC) for s in SEATED] for y in range(NY)]


def hop_y(array, step):
    count = NY * RING
    return lax.ppermute(array, AXES, [(d, (d + RING * step) % count) for d in range(count)])


def hop_core(array):
    return lax.ppermute(array, AXES, [(d, d ^ SHARDS) for d in range(NY * RING)])


LANES = 128


def put_dense(out, index, block):
    n, columns = block.shape
    whole = columns // LANES
    for tile in range(whole):
        out[index, tile * n : (tile + 1) * n] = block[:, tile * LANES : (tile + 1) * LANES]
    rest = block[:, whole * LANES :]
    out[index, whole * n :] = jnp.concatenate([rest[: n // 2], rest[n // 2 :]], axis=1)


def get_dense(blocks, index, n):
    whole = blocks.shape[1] // n
    tiles = [blocks[index, tile * n : (tile + 1) * n] for tile in range(whole)]
    rest = blocks[index, whole * n :]
    return tiles + [jnp.concatenate([rest[:, : LANES // 2], rest[:, LANES // 2 :]], axis=0)]


def dense_rows(n, columns):
    return n * columns // LANES


def pack_kernel(owners, group, grads, out, rows, places, sems):
    count, unroll = owners.shape[0], 8

    def copy(m, k):
        return pltpu.make_async_copy(grads.at[m], rows.at[k], sems.at[k])

    def look(m, found):
        owner = owners[m]
        mine = (owner >> 5) == group[0]

        @pl.when(mine)
        def _():
            copy(m, found).start()
            places[found] = seat((owner >> 2) & (NZ - 1), owner & (NX - 1))

        return found + mine.astype(jnp.int32)

    def look_many(i, found):
        for j in range(unroll):
            found = look(i * unroll + j, found)
        return found

    found = lax.fori_loop(0, count // unroll, look_many, jnp.int32(0))
    for m in range(count // unroll * unroll, count):
        found = look(m, found)

    def store(k, carry):
        copy(0, k).wait()
        put_dense(out, places[k], rows[k])
        return carry

    lax.fori_loop(0, found, store, 0)


def pack(owners, group, grads):
    _, rows, columns = grads.shape
    return pl.pallas_call(
        pack_kernel,
        out_shape=jax.ShapeDtypeStruct((SHARDS, dense_rows(rows, columns), LANES), grads.dtype),
        in_specs=[SMEM, SMEM, HBM],
        out_specs=VMEM,
        scratch_shapes=[
            pltpu.VMEM((SHARDS, rows, columns), grads.dtype),
            pltpu.SMEM((SHARDS,), jnp.int32),
            pltpu.SemaphoreType.DMA((SHARDS,)),
        ],
        compiler_params=pltpu.CompilerParams(vmem_limit_bytes=56 * 2**20),
        name="pack_rows",
    )(owners, group, grads)


def dot(a, b, dims):
    return lax.dot_general(a, b, dims, preferred_element_type=jnp.float32)


def step_kernel(scale, owned_ref, rows_ref, mom_ref, out_ref, next_ref, blend, cur, gram, poly):
    rows = mom_ref.shape[1] // SHARDS
    half = rows // NC
    span = NX * rows
    owned = owned_ref[0] > 0
    total = jnp.zeros((8, span), jnp.float32)
    for z in range(NZ):
        cols = slice(z * span, (z + 1) * span)
        tiles = zip(*[get_dense(rows_ref, seat(z, x), rows) for x in range(NX)])
        grad = jnp.concatenate([jnp.concatenate(tile, axis=0) for tile in tiles], axis=1)
        grad = jnp.where(owned, grad.T.astype(jnp.float32), 0.0)
        renewed = DECAY * mom_ref[:, cols].astype(jnp.float32) + grad
        next_ref[:, cols] = renewed.astype(jnp.bfloat16)
        mixed = grad + DECAY * renewed
        blend[:, cols] = mixed
        total = total + jnp.sum((mixed * mixed).reshape(-1, 8, span), axis=0)
    inverse = 1.0 / (jnp.sqrt(jnp.sum(total)) + EPS)
    cur[...] = (blend[...] * inverse).astype(jnp.bfloat16)
    columns, total_rows = cur.shape
    cuts = [(low, min(low + 256, columns)) for low in range(0, columns, 256)]
    wide = 2 * span
    for iteration in range(ITERS):
        for low, high in cuts:
            block = dot(cur[:high], cur[low:high], NT).astype(jnp.bfloat16)
            gram[:high, low:high] = block
            if low:
                gram[low:high, :low] = block[:low].T
        for low, high in cuts:
            square = dot(gram[:high], gram[:, low:high], NN)
            block = (CUBIC * gram[:high, low:high].astype(jnp.float32) + QUINTIC * square).astype(jnp.bfloat16)
            poly[:high, low:high] = block
            if low:
                poly[low:high, :low] = block[:low].T
        factor = poly[...]
        if iteration + 1 < ITERS:
            x = cur[...]
            cur[...] = (LINEAR * x.astype(jnp.float32) + dot(factor, x, NN)).astype(jnp.bfloat16)
            continue
        for left in range(0, total_rows, wide):
            x = cur[:, left : left + wide]
            last = (scale * LINEAR) * x.astype(jnp.float32) + scale * dot(factor, x, NN)
            last = last.astype(jnp.bfloat16)
            for z in range(left // span, (left + wide) // span):
                update = last[:, z * span - left : (z + 1) * span - left].T
                for x in range(NX):
                    for c in range(NC):
                        low = x * rows + c * half
                        out_ref[c * SHARDS + seat(z, x)] = update[low : low + half]


def muon_step(owned, rows, momentum_t):
    columns, total_rows = momentum_t.shape
    scale = 0.2 * math.sqrt(max(columns, total_rows))
    square = pltpu.VMEM((columns, columns), jnp.bfloat16)
    return pl.pallas_call(
        functools.partial(step_kernel, scale),
        out_shape=(
            jax.ShapeDtypeStruct((RING, total_rows // RING, columns), jnp.bfloat16),
            jax.ShapeDtypeStruct(momentum_t.shape, jnp.bfloat16),
        ),
        in_specs=[SMEM, VMEM, VMEM],
        out_specs=(VMEM, VMEM),
        scratch_shapes=[
            pltpu.VMEM(momentum_t.shape, jnp.float32),
            pltpu.VMEM(momentum_t.shape, jnp.bfloat16),
            square,
            square,
        ],
        compiler_params=pltpu.CompilerParams(vmem_limit_bytes=48 * 2**20),
        name="newton_schulz",
    )(owned, rows, momentum_t)


def select_kernel(seats, order, counts, where, blocks, low, high):
    y = where[0]
    split = low.shape[0]
    for out, first, last in ((low, 0, jnp.minimum(counts[y], split)), (high, split, counts[y])):

        def body(k, carry):
            out[k - first] = blocks[seats[order[y * RING + k]]]
            return carry

        lax.fori_loop(first, last, body, 0)


def select(seats, order, counts, where, blocks, slots):
    out = jax.ShapeDtypeStruct((slots // 2,) + blocks.shape[1:], blocks.dtype)
    return pl.pallas_call(
        select_kernel,
        out_shape=(out, out),
        in_specs=[SMEM] * 4 + [VMEM],
        out_specs=(VMEM, VMEM),
        name="select_blocks",
    )(seats, order, counts, where, blocks)


def place_kernel(origins, order, counts, where, *refs):
    pieces, out, sems = refs[: len(origins)], refs[-2], refs[-1]
    y, c = where[0], where[1]
    half = out.shape[1] // NC
    for run in ("start", "wait"):
        for (core, hop, first), piece in zip(origins, pieces):
            low = pl.multiple_of((c ^ core) * half, half)
            home = (y + hop) & (NY - 1)

            def body(k, carry):
                m = order[home * RING + k]
                copy = pltpu.make_async_copy(
                    piece.at[k - first], out.at[m, pl.ds(low, half)], sems.at[core, m]
                )
                getattr(copy, run)()
                return carry

            lax.fori_loop(first, jnp.minimum(counts[home], first + piece.shape[0]), body, 0)


def place(origins, order, counts, where, pieces, count, base=None):
    _, half, columns = pieces[0].shape
    bases = [] if base is None else [base]
    return pl.pallas_call(
        functools.partial(place_kernel, origins),
        out_shape=jax.ShapeDtypeStruct((count, NC * half, columns), pieces[0].dtype),
        in_specs=[SMEM] * 3 + [VMEM] * len(pieces) + [HBM] * len(bases),
        out_specs=HBM,
        input_output_aliases={3 + len(pieces): 0} if bases else {},
        scratch_shapes=[pltpu.SemaphoreType.DMA((NC, count))],
        compiler_params=pltpu.CompilerParams(vmem_limit_bytes=16 * 2**20),
        name="place_blocks",
    )(order, counts, where, *pieces, *bases)


def spread(slots, seats, order, counts, where, blocks):
    count = seats.shape[0]
    split = slots // 2
    low, high = select(seats, order, counts, where, blocks, slots)
    below_low, above_high = hop_y(low, 1), hop_y(high, -1)
    below_high, above_low = hop_y(high, 1), hop_y(low, -1)
    far = [hop_y(below_low, 1), hop_y(above_high, -1)]
    early = lax.optimization_barrier([low, high, below_low, above_high])
    early += [hop_core(piece) for piece in early]
    origins = [(core, *origin) for core in range(NC) for origin in ((0, 0), (0, split), (3, 0), (1, split))]
    updates = place(origins, order, counts, where, early, count)
    late = lax.optimization_barrier([below_high, above_low] + far)
    late += [hop_core(piece) for piece in late]
    origins = [(core, *origin) for core in range(NC) for origin in ((3, split), (1, 0), (2, 0), (2, split))]
    return place(origins, order, counts, where, late, count, updates)


def on_device(grads, momentum, owners):
    count = owners.shape[0]
    group = lax.axis_index("dp")
    me = lax.axis_index(AXES)
    where = jnp.stack([me // RING, me // SHARDS % NC]).astype(jnp.int32)
    packed = pack(owners, group[None].astype(jnp.int32), grads)
    rows = lax.all_to_all(packed, AXES, 0, 0, tiled=True, axis_index_groups=GROUPS_32)

    ids = jnp.arange(count, dtype=jnp.int32)
    homes = owners // RING
    seats = (owners & SHARDS) + seat((owners >> 2) & (NZ - 1), owners & (NX - 1))
    before = (homes[:, None] == homes[None, :]) & (owners[None, :] < owners[:, None])
    slot = homes * RING + jnp.sum(before.astype(jnp.int32), axis=1)
    order = jnp.sum(
        jnp.where(slot[None, :] == jnp.arange(NY * RING, dtype=jnp.int32)[:, None], ids[None, :], 0), axis=1
    )
    counts = jnp.sum((homes[None, :] == jnp.arange(NY, dtype=jnp.int32)[:, None]).astype(jnp.int32), axis=1)
    owned = jnp.any(owners == me)[None].astype(jnp.int32)

    blocks, following = muon_step(owned, rows, momentum[0].T)
    blocks = lax.all_to_all(blocks, AXES, 0, 0, tiled=True, axis_index_groups=GROUPS_64)
    few = 34
    updates = lax.cond(
        jnp.max(counts) <= few,
        functools.partial(spread, few),
        functools.partial(spread, RING),
        seats,
        order,
        counts,
        where,
        blocks,
    )
    return (updates, following.T[None])


def solution(mesh):
    return jax.shard_map(
        on_device,
        mesh=mesh,
        in_specs=(P(None, "shard", None), P(AXES, None, None), P()),
        out_specs=(P(None, "shard", None), P(AXES, None, None)),
        check_vma=False,
    )
```

```python
import functools
import math

import jax
import jax.numpy as jnp
from jax import lax
from jax.experimental import pallas as pl
from jax.experimental.pallas import tpu as pltpu
from jax.sharding import PartitionSpec as P

DECAY = 0.95
LINEAR, CUBIC, QUINTIC = 3.4445, -4.775, 2.0315
EPS = 1e-07
ITERS = 2
AXES = ("dp", "shard")
NZ, NX, NC, NY = 8, 4, 2, 4
SHARDS = NZ * NX
RING = NC * SHARDS
NT = (((1,), (1,)), ((), ()))
NN = (((1,), (0,)), ((), ()))
ANY = pl.BlockSpec(memory_space=pl.ANY)
HBM = pl.BlockSpec(memory_space=pltpu.HBM)
SMEM = pl.BlockSpec(memory_space=pltpu.SMEM)
VMEM = pl.BlockSpec(memory_space=pltpu.VMEM)


def seat(z, x):
    pick = jnp.where if isinstance(z, jax.Array) else (lambda c, a, b: a if c else b)
    return pick(z < NZ // 2, 2 * z, 2 * NZ - 1 - 2 * z) + NZ * pick(x < NX // 2, 2 * x, 2 * NX - 1 - 2 * x)


SEATED = sorted(range(SHARDS), key=lambda s: seat(s // NX, s % NX))
GROUPS_32 = [[g * SHARDS + s for s in SEATED] for g in range(NY * NC)]
GROUPS_64 = [[y * RING + c * SHARDS + s for c in range(NC) for s in SEATED] for y in range(NY)]


def hop_y(array, step):
    count = NY * RING
    return lax.ppermute(array, AXES, [(d, (d + RING * step) % count) for d in range(count)])


def hop_core(array):
    return lax.ppermute(array, AXES, [(d, d ^ SHARDS) for d in range(NY * RING)])


LANES = 128


def put_dense(out, index, block):
    n, columns = block.shape
    whole = columns // LANES
    for tile in range(whole):
        out[index, tile * n : (tile + 1) * n] = block[:, tile * LANES : (tile + 1) * LANES]
    rest = block[:, whole * LANES :]
    out[index, whole * n :] = jnp.concatenate([rest[: n // 2], rest[n // 2 :]], axis=1)


def get_dense(blocks, index, n):
    whole = blocks.shape[1] // n
    tiles = [blocks[index, tile * n : (tile + 1) * n] for tile in range(whole)]
    rest = blocks[index, whole * n :]
    return tiles + [jnp.concatenate([rest[:, : LANES // 2], rest[:, LANES // 2 :]], axis=0)]


def dense_rows(n, columns):
    return n * columns // LANES


def pack_kernel(owners, group, grads, out, rows, places, sems):
    count, unroll = owners.shape[0], 8

    def copy(m, k):
        return pltpu.make_async_copy(grads.at[m], rows.at[k], sems.at[k])

    def look(m, found):
        owner = owners[m]
        mine = (owner >> 5) == group[0]

        @pl.when(mine)
        def _():
            copy(m, found).start()
            places[found] = seat((owner >> 2) & (NZ - 1), owner & (NX - 1))

        return found + mine.astype(jnp.int32)

    def look_many(i, found):
        for j in range(unroll):
            found = look(i * unroll + j, found)
        return found

    found = lax.fori_loop(0, count // unroll, look_many, jnp.int32(0))
    for m in range(count // unroll * unroll, count):
        found = look(m, found)

    def store(k, carry):
        copy(0, k).wait()
        put_dense(out, places[k], rows[k])
        return carry

    lax.fori_loop(0, found, store, 0)


def pack(owners, group, grads):
    _, rows, columns = grads.shape
    return pl.pallas_call(
        pack_kernel,
        out_shape=jax.ShapeDtypeStruct((SHARDS, dense_rows(rows, columns), LANES), grads.dtype),
        in_specs=[SMEM, SMEM, HBM],
        out_specs=VMEM,
        scratch_shapes=[
            pltpu.VMEM((SHARDS, rows, columns), grads.dtype),
            pltpu.SMEM((SHARDS,), jnp.int32),
            pltpu.SemaphoreType.DMA((SHARDS,)),
        ],
        compiler_params=pltpu.CompilerParams(vmem_limit_bytes=56 * 2**20),
        name="pack_rows",
    )(owners, group, grads)


def dot(a, b, dims):
    return lax.dot_general(a, b, dims, preferred_element_type=jnp.float32)


def step_kernel(scale, owned_ref, rows_ref, mom_ref, out_ref, next_ref, blend, cur, gram, poly):
    rows = mom_ref.shape[1] // SHARDS
    half = rows // NC
    span = NX * rows
    owned = owned_ref[0] > 0
    total = jnp.zeros((8, span), jnp.float32)
    for z in range(NZ):
        cols = slice(z * span, (z + 1) * span)
        tiles = zip(*[get_dense(rows_ref, seat(z, x), rows) for x in range(NX)])
        grad = jnp.concatenate([jnp.concatenate(tile, axis=0) for tile in tiles], axis=1)
        grad = jnp.where(owned, grad.T.astype(jnp.float32), 0.0)
        renewed = DECAY * mom_ref[:, cols].astype(jnp.float32) + grad
        next_ref[:, cols] = renewed.astype(jnp.bfloat16)
        mixed = grad + DECAY * renewed
        blend[:, cols] = mixed
        total = total + jnp.sum((mixed * mixed).reshape(-1, 8, span), axis=0)
    inverse = 1.0 / (jnp.sqrt(jnp.sum(total)) + EPS)
    cur[...] = (blend[...] * inverse).astype(jnp.bfloat16)
    columns, total_rows = cur.shape
    cuts = [(low, min(low + 256, columns)) for low in range(0, columns, 256)]
    wide = 2 * span
    for iteration in range(ITERS):
        for low, high in cuts:
            block = dot(cur[:high], cur[low:high], NT).astype(jnp.bfloat16)
            gram[:high, low:high] = block
            if low:
                gram[low:high, :low] = block[:low].T
        for low, high in cuts:
            square = dot(gram[:high], gram[:, low:high], NN)
            block = (CUBIC * gram[:high, low:high].astype(jnp.float32) + QUINTIC * square).astype(jnp.bfloat16)
            poly[:high, low:high] = block
            if low:
                poly[low:high, :low] = block[:low].T
        factor = poly[...]
        if iteration + 1 < ITERS:
            x = cur[...]
            cur[...] = (LINEAR * x.astype(jnp.float32) + dot(factor, x, NN)).astype(jnp.bfloat16)
            continue
        for left in range(0, total_rows, wide):
            x = cur[:, left : left + wide]
            last = (scale * LINEAR) * x.astype(jnp.float32) + scale * dot(factor, x, NN)
            last = last.astype(jnp.bfloat16)
            for z in range(left // span, (left + wide) // span):
                update = last[:, z * span - left : (z + 1) * span - left].T
                for x in range(NX):
                    for c in range(NC):
                        low = x * rows + c * half
                        out_ref[c * SHARDS + seat(z, x)] = update[low : low + half]


def muon_step(owned, rows, momentum_t):
    columns, total_rows = momentum_t.shape
    scale = 0.2 * math.sqrt(max(columns, total_rows))
    square = pltpu.VMEM((columns, columns), jnp.bfloat16)
    return pl.pallas_call(
        functools.partial(step_kernel, scale),
        out_shape=(
            jax.ShapeDtypeStruct((RING, total_rows // RING, columns), jnp.bfloat16),
            jax.ShapeDtypeStruct(momentum_t.shape, jnp.bfloat16),
        ),
        in_specs=[SMEM, VMEM, VMEM],
        out_specs=(VMEM, VMEM),
        scratch_shapes=[
            pltpu.VMEM(momentum_t.shape, jnp.float32),
            pltpu.VMEM(momentum_t.shape, jnp.bfloat16),
            square,
            square,
        ],
        compiler_params=pltpu.CompilerParams(vmem_limit_bytes=48 * 2**20),
        name="newton_schulz",
    )(owned, rows, momentum_t)


def select_kernel(seats, order, counts, where, blocks, out):
    y = where[0]

    def body(k, carry):
        out[k] = blocks[seats[order[y * RING + k]]]
        return carry

    lax.fori_loop(0, counts[y], body, 0)


def select(seats, order, counts, where, blocks, slots):
    return pl.pallas_call(
        select_kernel,
        out_shape=jax.ShapeDtypeStruct((slots,) + blocks.shape[1:], blocks.dtype),
        in_specs=[SMEM] * 4 + [VMEM],
        out_specs=VMEM,
        compiler_params=pltpu.CompilerParams(vmem_limit_bytes=16 * 2**20),
        name="select_blocks",
    )(seats, order, counts, where, blocks)


def place_kernel(origins, order, counts, where, *refs):
    pieces, out, sems = refs[: len(origins)], refs[-2], refs[-1]
    y, c = where[0], where[1]
    half = out.shape[1] // NC
    for run in ("start", "wait"):
        for (core, hop, first), piece in zip(origins, pieces):
            low = pl.multiple_of((c ^ core) * half, half)
            home = (y + hop) & (NY - 1)

            def body(k, carry):
                m = order[home * RING + k]
                copy = pltpu.make_async_copy(
                    piece.at[k - first], out.at[m, pl.ds(low, half)], sems.at[core, m]
                )
                getattr(copy, run)()
                return carry

            def four(i, carry):
                for j in range(4):
                    body(first + 4 * i + j, 0)
                return carry

            last = jnp.minimum(counts[home], first + piece.shape[0])
            fours = jnp.maximum(last - first, 0) >> 2
            lax.fori_loop(0, fours, four, 0)
            lax.fori_loop(first + 4 * fours, last, body, 0)


def place(origins, order, counts, where, pieces, count, base=None):
    _, half, columns = pieces[0].shape
    bases = [] if base is None else [base]
    return pl.pallas_call(
        functools.partial(place_kernel, origins),
        out_shape=jax.ShapeDtypeStruct((count, NC * half, columns), pieces[0].dtype),
        in_specs=[SMEM] * 3 + [VMEM] * len(pieces) + [HBM] * len(bases),
        out_specs=HBM,
        input_output_aliases={3 + len(pieces): 0} if bases else {},
        scratch_shapes=[pltpu.SemaphoreType.DMA((NC, count))],
        compiler_params=pltpu.CompilerParams(vmem_limit_bytes=16 * 2**20),
        name="place_blocks",
    )(order, counts, where, *pieces, *bases)


def spread(slots, seats, order, counts, where, blocks):
    count = seats.shape[0]
    split = slots // 2
    own = select(seats, order, counts, where, blocks, slots)
    low, high = own[:split], own[split:]
    below_low, above_high = hop_y(low, 1), hop_y(high, -1)
    below_high, above_low = hop_y(high, 1), hop_y(low, -1)
    far = [hop_y(below_low, 1), hop_y(above_high, -1)]
    early = [own, below_low, above_high]
    early += [hop_core(piece) for piece in early]
    origins = [(core, *origin) for core in range(NC) for origin in ((0, 0), (3, 0), (1, split))]
    updates = place(origins, order, counts, where, early, count)
    late = lax.optimization_barrier([below_high, above_low] + far)
    late += [hop_core(piece) for piece in late]
    origins = [(core, *origin) for core in range(NC) for origin in ((3, split), (1, 0), (2, 0), (2, split))]
    return place(origins, order, counts, where, late, count, updates)


def on_device(grads, momentum, owners):
    count = owners.shape[0]
    group = lax.axis_index("dp")
    me = lax.axis_index(AXES)
    where = jnp.stack([me // RING, me // SHARDS % NC]).astype(jnp.int32)
    packed = pack(owners, group[None].astype(jnp.int32), grads)
    rows = lax.all_to_all(packed, AXES, 0, 0, tiled=True, axis_index_groups=GROUPS_32)

    ids = jnp.arange(count, dtype=jnp.int32)
    homes = owners // RING
    seats = (owners & SHARDS) + seat((owners >> 2) & (NZ - 1), owners & (NX - 1))
    before = (homes[:, None] == homes[None, :]) & (owners[None, :] < owners[:, None])
    slot = homes * RING + jnp.sum(before.astype(jnp.int32), axis=1)
    order = jnp.sum(
        jnp.where(slot[None, :] == jnp.arange(NY * RING, dtype=jnp.int32)[:, None], ids[None, :], 0), axis=1
    )
    counts = jnp.sum((homes[None, :] == jnp.arange(NY, dtype=jnp.int32)[:, None]).astype(jnp.int32), axis=1)
    owned = jnp.any(owners == me)[None].astype(jnp.int32)

    blocks, following = muon_step(owned, rows, momentum[0].T)
    blocks = lax.all_to_all(blocks, AXES, 0, 0, tiled=True, axis_index_groups=GROUPS_64)
    few = 34
    updates = lax.cond(
        jnp.max(counts) <= few,
        functools.partial(spread, few),
        functools.partial(spread, RING),
        seats,
        order,
        counts,
        where,
        blocks,
    )
    return (updates, following.T[None])


def solution(mesh):
    return jax.shard_map(
        on_device,
        mesh=mesh,
        in_specs=(P(None, "shard", None), P(AXES, None, None), P()),
        out_specs=(P(None, "shard", None), P(AXES, None, None)),
        check_vma=False,
    )
```

```python
import functools
import math

import jax
import jax.numpy as jnp
from jax import lax
from jax.experimental import pallas as pl
from jax.experimental.pallas import tpu as pltpu
from jax.sharding import PartitionSpec as P

DECAY = 0.95
LINEAR, CUBIC, QUINTIC = 3.4445, -4.775, 2.0315
EPS = 1e-07
ITERS = 2
AXES = ("dp", "shard")
NZ, NX, NC, NY = 8, 4, 2, 4
SHARDS = NZ * NX
GROUPS = NY * NC
NT = (((1,), (1,)), ((), ()))
NN = (((1,), (0,)), ((), ()))
ANY = pl.BlockSpec(memory_space=pl.ANY)
HBM = pl.BlockSpec(memory_space=pltpu.HBM)
SMEM = pl.BlockSpec(memory_space=pltpu.SMEM)
VMEM = pl.BlockSpec(memory_space=pltpu.VMEM)


def seat(z, x):
    pick = jnp.where if isinstance(z, jax.Array) else (lambda c, a, b: a if c else b)
    return pick(z < NZ // 2, 2 * z, 2 * NZ - 1 - 2 * z) + NZ * pick(x < NX // 2, 2 * x, 2 * NX - 1 - 2 * x)


SEATED = sorted(range(SHARDS), key=lambda s: seat(s // NX, s % NX))
MEMBERS = [[g * SHARDS + s for s in SEATED] for g in range(GROUPS)]


def hop_y(array, step):
    count, along = GROUPS * SHARDS, NC * SHARDS
    return lax.ppermute(array, AXES, [(d, (d + along * step) % count) for d in range(count)])


def hop_core(array):
    return lax.ppermute(array, AXES, [(d, d ^ SHARDS) for d in range(GROUPS * SHARDS)])


LANES = 128


def put_dense(out, index, block):
    n, columns = block.shape
    whole = columns // LANES
    for tile in range(whole):
        out[index, tile * n : (tile + 1) * n] = block[:, tile * LANES : (tile + 1) * LANES]
    rest = block[:, whole * LANES :]
    out[index, whole * n :] = jnp.concatenate([rest[: n // 2], rest[n // 2 :]], axis=1)


def get_dense(blocks, index, n):
    whole = blocks.shape[1] // n
    tiles = [blocks[index, tile * n : (tile + 1) * n] for tile in range(whole)]
    rest = blocks[index, whole * n :]
    return tiles + [jnp.concatenate([rest[:, : LANES // 2], rest[:, LANES // 2 :]], axis=0)]


def dense_rows(n, columns):
    return n * columns // LANES


def pack_kernel(owners, group, grads, out, rows, places, sems):
    count, unroll = owners.shape[0], 8

    def copy(m, k):
        return pltpu.make_async_copy(grads.at[m], rows.at[k], sems.at[k])

    def look(m, found):
        owner = owners[m]
        mine = (owner >> 5) == group[0]

        @pl.when(mine)
        def _():
            copy(m, found).start()
            places[found] = seat((owner >> 2) & (NZ - 1), owner & (NX - 1))

        return found + mine.astype(jnp.int32)

    def look_many(i, found):
        for j in range(unroll):
            found = look(i * unroll + j, found)
        return found

    found = lax.fori_loop(0, count // unroll, look_many, jnp.int32(0))
    for m in range(count // unroll * unroll, count):
        found = look(m, found)

    def store(k, carry):
        copy(0, k).wait()
        put_dense(out, places[k], rows[k])
        return carry

    lax.fori_loop(0, found, store, 0)


def pack(owners, group, grads):
    _, rows, columns = grads.shape
    return pl.pallas_call(
        pack_kernel,
        out_shape=jax.ShapeDtypeStruct((SHARDS, dense_rows(rows, columns), LANES), grads.dtype),
        in_specs=[SMEM, SMEM, HBM],
        out_specs=VMEM,
        scratch_shapes=[
            pltpu.VMEM((SHARDS, rows, columns), grads.dtype),
            pltpu.SMEM((SHARDS,), jnp.int32),
            pltpu.SemaphoreType.DMA((SHARDS,)),
        ],
        compiler_params=pltpu.CompilerParams(vmem_limit_bytes=56 * 2**20),
        name="pack_rows",
    )(owners, group, grads)


def dot(a, b, dims):
    return lax.dot_general(a, b, dims, preferred_element_type=jnp.float32)


def step_kernel(scale, owned_ref, rows_ref, mom_ref, out_ref, next_ref, blend, cur, gram, poly):
    rows = mom_ref.shape[1] // SHARDS
    span = NX * rows
    owned = owned_ref[0] > 0
    total = jnp.zeros((8, span), jnp.float32)
    for z in range(NZ):
        cols = slice(z * span, (z + 1) * span)
        tiles = zip(*[get_dense(rows_ref, seat(z, x), rows) for x in range(NX)])
        grad = jnp.concatenate([jnp.concatenate(tile, axis=0) for tile in tiles], axis=1)
        grad = jnp.where(owned, grad.T.astype(jnp.float32), 0.0)
        renewed = DECAY * mom_ref[:, cols].astype(jnp.float32) + grad
        next_ref[:, cols] = renewed.astype(jnp.bfloat16)
        mixed = grad + DECAY * renewed
        blend[:, cols] = mixed
        total = total + jnp.sum((mixed * mixed).reshape(-1, 8, span), axis=0)
    inverse = 1.0 / (jnp.sqrt(jnp.sum(total)) + EPS)
    cur[...] = (blend[...] * inverse).astype(jnp.bfloat16)
    columns, total_rows = cur.shape
    cuts = [(low, min(low + 256, columns)) for low in range(0, columns, 256)]
    wide = 2 * span
    for iteration in range(ITERS):
        for low, high in cuts:
            block = dot(cur[:high], cur[low:high], NT).astype(jnp.bfloat16)
            gram[:high, low:high] = block
            if low:
                gram[low:high, :low] = block[:low].T
        for low, high in cuts:
            square = dot(gram[:high], gram[:, low:high], NN)
            block = (CUBIC * gram[:high, low:high].astype(jnp.float32) + QUINTIC * square).astype(jnp.bfloat16)
            poly[:high, low:high] = block
            if low:
                poly[low:high, :low] = block[:low].T
        factor = poly[...]
        if iteration + 1 < ITERS:
            x = cur[...]
            cur[...] = (LINEAR * x.astype(jnp.float32) + dot(factor, x, NN)).astype(jnp.bfloat16)
            continue
        for left in range(0, total_rows, wide):
            x = cur[:, left : left + wide]
            last = (scale * LINEAR) * x.astype(jnp.float32) + scale * dot(factor, x, NN)
            last = last.astype(jnp.bfloat16)
            for z in range(left // span, (left + wide) // span):
                update = last[:, z * span - left : (z + 1) * span - left].T
                for x in range(NX):
                    put_dense(out_ref, seat(z, x), update[x * rows : (x + 1) * rows])


def muon_step(owned, rows, momentum_t):
    columns, total_rows = momentum_t.shape
    scale = 0.2 * math.sqrt(max(columns, total_rows))
    square = pltpu.VMEM((columns, columns), jnp.bfloat16)
    return pl.pallas_call(
        functools.partial(step_kernel, scale),
        out_shape=(
            jax.ShapeDtypeStruct(rows.shape, jnp.bfloat16),
            jax.ShapeDtypeStruct(momentum_t.shape, jnp.bfloat16),
        ),
        in_specs=[SMEM, VMEM, VMEM],
        out_specs=(VMEM, VMEM),
        scratch_shapes=[
            pltpu.VMEM(momentum_t.shape, jnp.float32),
            pltpu.VMEM(momentum_t.shape, jnp.bfloat16),
            square,
            square,
        ],
        compiler_params=pltpu.CompilerParams(vmem_limit_bytes=48 * 2**20),
        name="newton_schulz",
    )(owned, rows, momentum_t)


def select_kernel(seats, order, counts, where, blocks, out):
    group = where[0]

    def body(k, carry):
        out[k] = blocks[seats[order[group * SHARDS + k]]]
        return carry

    lax.fori_loop(0, counts[group], body, 0)


def select(seats, order, counts, where, blocks, slots):
    return pl.pallas_call(
        select_kernel,
        out_shape=jax.ShapeDtypeStruct((slots,) + blocks.shape[1:], blocks.dtype),
        in_specs=[SMEM] * 4 + [VMEM],
        out_specs=VMEM,
        compiler_params=pltpu.CompilerParams(vmem_limit_bytes=16 * 2**20),
        name="select_blocks",
    )(seats, order, counts, where, blocks)


def place_kernel(origins, order, counts, where, *refs):
    pieces, (out, rows, sems) = refs[: len(origins)], refs[-3:]
    height = out.shape[1]
    offsets = [sum(piece.shape[0] for piece in pieces[:i]) for i in range(len(pieces))]

    def unpack(chosen, k, carry):
        for i in chosen:
            for tile, value in enumerate(get_dense(pieces[i], k, height)):
                left = tile * LANES
                rows[offsets[i] + k, :, left : left + value.shape[1]] = value
        return carry

    done = 0
    for size in sorted({piece.shape[0] for piece in pieces}):
        chosen = [i for i, piece in enumerate(pieces) if piece.shape[0] >= size]
        lax.fori_loop(done, size, functools.partial(unpack, chosen), 0)
        done = size

    for run in ("start", "wait"):
        for (core, hop, first), piece, offset in zip(origins, pieces, offsets):
            home = (where[0] ^ core) + NC * hop & (GROUPS - 1)

            def body(k, carry):
                m = order[home * SHARDS + k]
                copy = pltpu.make_async_copy(rows.at[offset + k - first], out.at[m], sems.at[m])
                getattr(copy, run)()
                return carry

            def four(i, carry):
                for j in range(4):
                    body(first + 4 * i + j, 0)
                return carry

            last = jnp.minimum(counts[home], first + piece.shape[0])
            fours = jnp.maximum(last - first, 0) >> 2
            lax.fori_loop(0, fours, four, 0)
            lax.fori_loop(first + 4 * fours, last, body, 0)


def place(origins, order, counts, where, pieces, shape, base=None):
    bases = [] if base is None else [base]
    slots = sum(piece.shape[0] for piece in pieces)
    return pl.pallas_call(
        functools.partial(place_kernel, origins),
        out_shape=jax.ShapeDtypeStruct(shape, pieces[0].dtype),
        in_specs=[SMEM] * 3 + [VMEM] * len(pieces) + [HBM] * len(bases),
        out_specs=HBM,
        input_output_aliases={3 + len(pieces): 0} if bases else {},
        scratch_shapes=[
            pltpu.VMEM((slots,) + shape[1:], pieces[0].dtype),
            pltpu.SemaphoreType.DMA((shape[0],)),
        ],
        compiler_params=pltpu.CompilerParams(vmem_limit_bytes=16 * 2**20),
        name="place_blocks",
    )(order, counts, where, *pieces, *bases)


def spread(slots, shape, seats, order, counts, where, blocks):
    split = (slots + 1) // 2
    own = select(seats, order, counts, where, blocks, slots)
    low, high = own[:split], own[split:]
    below_low, above_high = hop_y(low, 1), hop_y(high, -1)
    below_high, above_low = hop_y(high, 1), hop_y(low, -1)
    far = [hop_y(below_low, 1), hop_y(above_high, -1)]
    early = [own, below_low, above_high]
    early += [hop_core(piece) for piece in early]
    origins = [(core, *origin) for core in range(NC) for origin in ((0, 0), (3, 0), (1, split))]
    updates = place(origins, order, counts, where, early, shape)
    late = lax.optimization_barrier([below_high, above_low] + far)
    late += [hop_core(piece) for piece in late]
    origins = [(core, *origin) for core in range(NC) for origin in ((3, split), (1, 0), (2, 0), (2, split))]
    return place(origins, order, counts, where, late, shape, updates)


def on_device(grads, momentum, owners):
    count = owners.shape[0]
    group = lax.axis_index("dp")
    me = lax.axis_index(AXES)
    where = group[None].astype(jnp.int32)
    packed = pack(owners, where, grads)
    rows = lax.all_to_all(packed, AXES, 0, 0, tiled=True, axis_index_groups=MEMBERS)

    ids = jnp.arange(count, dtype=jnp.int32)
    homes = owners // SHARDS
    seats = seat((owners >> 2) & (NZ - 1), owners & (NX - 1))
    before = (homes[:, None] == homes[None, :]) & (owners[None, :] < owners[:, None])
    slot = homes * SHARDS + jnp.sum(before.astype(jnp.int32), axis=1)
    order = jnp.sum(
        jnp.where(slot[None, :] == jnp.arange(GROUPS * SHARDS, dtype=jnp.int32)[:, None], ids[None, :], 0), axis=1
    )
    counts = jnp.sum((homes[None, :] == jnp.arange(GROUPS, dtype=jnp.int32)[:, None]).astype(jnp.int32), axis=1)
    owned = jnp.any(owners == me)[None].astype(jnp.int32)

    blocks, following = muon_step(owned, rows, momentum[0].T)
    blocks = lax.all_to_all(blocks, AXES, 0, 0, tiled=True, axis_index_groups=MEMBERS)
    few = 19
    updates = lax.cond(
        jnp.max(counts) <= few,
        functools.partial(spread, few, grads.shape),
        functools.partial(spread, SHARDS, grads.shape),
        seats,
        order,
        counts,
        where,
        blocks,
    )
    return (updates, following.T[None])


def solution(mesh):
    return jax.shard_map(
        on_device,
        mesh=mesh,
        in_specs=(P(None, "shard", None), P(AXES, None, None), P()),
        out_specs=(P(None, "shard", None), P(AXES, None, None)),
        check_vma=False,
    )
```

```python
import functools
import math

import jax
import jax.numpy as jnp
from jax import lax
from jax.experimental import pallas as pl
from jax.experimental.pallas import tpu as pltpu
from jax.sharding import PartitionSpec as P

DECAY = 0.95
LINEAR, CUBIC, QUINTIC = 3.4445, -4.775, 2.0315
EPS = 1e-07
ITERS = 2
AXES = ("dp", "shard")
NZ, NX, NC, NY = 8, 4, 2, 4
SHARDS = NZ * NX
GROUPS = NY * NC
NT = (((1,), (1,)), ((), ()))
NN = (((1,), (0,)), ((), ()))
ANY = pl.BlockSpec(memory_space=pl.ANY)
HBM = pl.BlockSpec(memory_space=pltpu.HBM)
SMEM = pl.BlockSpec(memory_space=pltpu.SMEM)
VMEM = pl.BlockSpec(memory_space=pltpu.VMEM)


def seat(z, x):
    pick = jnp.where if isinstance(z, jax.Array) else (lambda c, a, b: a if c else b)
    return pick(z < NZ // 2, 2 * z, 2 * NZ - 1 - 2 * z) + NZ * pick(x < NX // 2, 2 * x, 2 * NX - 1 - 2 * x)


SEATED = sorted(range(SHARDS), key=lambda s: seat(s // NX, s % NX))
MEMBERS = [[g * SHARDS + s for s in SEATED] for g in range(GROUPS)]


def hop_y(array, step):
    count, along = GROUPS * SHARDS, NC * SHARDS
    return lax.ppermute(array, AXES, [(d, (d + along * step) % count) for d in range(count)])


def hop_core(array):
    return lax.ppermute(array, AXES, [(d, d ^ SHARDS) for d in range(GROUPS * SHARDS)])


LANES = 128


def put_dense(out, index, block):
    n, columns = block.shape
    whole = columns // LANES
    for tile in range(whole):
        out[index, tile * n : (tile + 1) * n] = block[:, tile * LANES : (tile + 1) * LANES]
    rest = block[:, whole * LANES :]
    out[index, whole * n :] = jnp.concatenate([rest[: n // 2], rest[n // 2 :]], axis=1)


def get_dense(blocks, index, n):
    whole = blocks.shape[1] // n
    tiles = [blocks[index, tile * n : (tile + 1) * n] for tile in range(whole)]
    rest = blocks[index, whole * n :]
    return tiles + [jnp.concatenate([rest[:, : LANES // 2], rest[:, LANES // 2 :]], axis=0)]


def dense_rows(n, columns):
    return n * columns // LANES


def pack_kernel(owners, group, grads, out, rows, places, sems):
    count, unroll = owners.shape[0], 8

    def copy(m, k):
        return pltpu.make_async_copy(grads.at[m], rows.at[k], sems.at[k])

    def look(m, found):
        owner = owners[m]
        mine = (owner >> 5) == group[0]

        @pl.when(mine)
        def _():
            copy(m, found).start()
            places[found] = seat((owner >> 2) & (NZ - 1), owner & (NX - 1))

        return found + mine.astype(jnp.int32)

    def look_many(i, found):
        for j in range(unroll):
            found = look(i * unroll + j, found)
        return found

    found = lax.fori_loop(0, count // unroll, look_many, jnp.int32(0))
    for m in range(count // unroll * unroll, count):
        found = look(m, found)

    def store(k, carry):
        copy(0, k).wait()
        put_dense(out, places[k], rows[k])
        return carry

    lax.fori_loop(0, found, store, 0)


def pack(owners, group, grads):
    _, rows, columns = grads.shape
    return pl.pallas_call(
        pack_kernel,
        out_shape=jax.ShapeDtypeStruct((SHARDS, dense_rows(rows, columns), LANES), grads.dtype),
        in_specs=[SMEM, SMEM, HBM],
        out_specs=VMEM,
        scratch_shapes=[
            pltpu.VMEM((SHARDS, rows, columns), grads.dtype),
            pltpu.SMEM((SHARDS,), jnp.int32),
            pltpu.SemaphoreType.DMA((SHARDS,)),
        ],
        compiler_params=pltpu.CompilerParams(vmem_limit_bytes=56 * 2**20),
        name="pack_rows",
    )(owners, group, grads)


def dot(a, b, dims):
    return lax.dot_general(a, b, dims, preferred_element_type=jnp.float32)


def step_kernel(scale, owned_ref, rows_ref, mom_ref, out_ref, next_hbm, blend, cur, gram, poly, next_ref, sem):
    rows = mom_ref.shape[1] // SHARDS
    span = NX * rows
    owned = owned_ref[0] > 0
    total = jnp.zeros((8, span), jnp.float32)
    for z in range(NZ):
        cols = slice(z * span, (z + 1) * span)
        tiles = zip(*[get_dense(rows_ref, seat(z, x), rows) for x in range(NX)])
        grad = jnp.concatenate([jnp.concatenate(tile, axis=0) for tile in tiles], axis=1)
        grad = jnp.where(owned, grad.T.astype(jnp.float32), 0.0)
        renewed = DECAY * mom_ref[:, cols].astype(jnp.float32) + grad
        next_ref[:, cols] = renewed.astype(jnp.bfloat16)
        mixed = grad + DECAY * renewed
        blend[:, cols] = mixed
        total = total + jnp.sum((mixed * mixed).reshape(-1, 8, span), axis=0)
    keep = pltpu.make_async_copy(next_ref, next_hbm, sem)
    keep.start()
    inverse = 1.0 / (jnp.sqrt(jnp.sum(total)) + EPS)
    cur[...] = (blend[...] * inverse).astype(jnp.bfloat16)
    columns, total_rows = cur.shape
    cuts = [(low, min(low + 256, columns)) for low in range(0, columns, 256)]
    wide = 2 * span
    for iteration in range(ITERS):
        for low, high in cuts:
            block = dot(cur[:high], cur[low:high], NT).astype(jnp.bfloat16)
            gram[:high, low:high] = block
            if low:
                gram[low:high, :low] = block[:low].T
        for low, high in cuts:
            square = dot(gram[:high], gram[:, low:high], NN)
            block = (CUBIC * gram[:high, low:high].astype(jnp.float32) + QUINTIC * square).astype(jnp.bfloat16)
            poly[:high, low:high] = block
            if low:
                poly[low:high, :low] = block[:low].T
        factor = poly[...]
        if iteration + 1 < ITERS:
            x = cur[...]
            cur[...] = (LINEAR * x.astype(jnp.float32) + dot(factor, x, NN)).astype(jnp.bfloat16)
            continue
        for left in range(0, total_rows, wide):
            x = cur[:, left : left + wide]
            last = (scale * LINEAR) * x.astype(jnp.float32) + scale * dot(factor, x, NN)
            last = last.astype(jnp.bfloat16)
            for z in range(left // span, (left + wide) // span):
                update = last[:, z * span - left : (z + 1) * span - left].T
                for x in range(NX):
                    put_dense(out_ref, seat(z, x), update[x * rows : (x + 1) * rows])
    keep.wait()


def muon_step(owned, rows, momentum_t):
    columns, total_rows = momentum_t.shape
    scale = 0.2 * math.sqrt(max(columns, total_rows))
    square = pltpu.VMEM((columns, columns), jnp.bfloat16)
    return pl.pallas_call(
        functools.partial(step_kernel, scale),
        out_shape=(
            jax.ShapeDtypeStruct(rows.shape, jnp.bfloat16),
            jax.ShapeDtypeStruct(momentum_t.shape, jnp.bfloat16),
        ),
        in_specs=[SMEM, VMEM, VMEM],
        out_specs=(VMEM, HBM),
        scratch_shapes=[
            pltpu.VMEM(momentum_t.shape, jnp.float32),
            pltpu.VMEM(momentum_t.shape, jnp.bfloat16),
            square,
            square,
            pltpu.VMEM(momentum_t.shape, jnp.bfloat16),
            pltpu.SemaphoreType.DMA,
        ],
        compiler_params=pltpu.CompilerParams(vmem_limit_bytes=48 * 2**20),
        name="newton_schulz",
    )(owned, rows, momentum_t)


def select_kernel(seats, order, counts, where, blocks, out):
    group = where[0]

    def body(k, carry):
        out[k] = blocks[seats[order[group * SHARDS + k]]]
        return carry

    lax.fori_loop(0, counts[group], body, 0)


def select(seats, order, counts, where, blocks, slots):
    return pl.pallas_call(
        select_kernel,
        out_shape=jax.ShapeDtypeStruct((slots,) + blocks.shape[1:], blocks.dtype),
        in_specs=[SMEM] * 4 + [VMEM],
        out_specs=VMEM,
        compiler_params=pltpu.CompilerParams(vmem_limit_bytes=16 * 2**20),
        name="select_blocks",
    )(seats, order, counts, where, blocks)


def place_kernel(origins, order, counts, where, *refs):
    pieces, (out, rows, sems) = refs[: len(origins)], refs[-3:]
    height = out.shape[1]
    offsets = [sum(piece.shape[0] for piece in pieces[:i]) for i in range(len(pieces))]

    def unpack(chosen, k, carry):
        for i in chosen:
            for tile, value in enumerate(get_dense(pieces[i], k, height)):
                left = tile * LANES
                rows[offsets[i] + k, :, left : left + value.shape[1]] = value
        return carry

    done = 0
    for size in sorted({piece.shape[0] for piece in pieces}):
        chosen = [i for i, piece in enumerate(pieces) if piece.shape[0] >= size]
        lax.fori_loop(done, size, functools.partial(unpack, chosen), 0)
        done = size

    for run in ("start", "wait"):
        for (core, hop, first), piece, offset in zip(origins, pieces, offsets):
            home = (where[0] ^ core) + NC * hop & (GROUPS - 1)

            def body(k, carry):
                m = order[home * SHARDS + k]
                copy = pltpu.make_async_copy(rows.at[offset + k - first], out.at[m], sems.at[m])
                getattr(copy, run)()
                return carry

            def four(i, carry):
                for j in range(4):
                    body(first + 4 * i + j, 0)
                return carry

            last = jnp.minimum(counts[home], first + piece.shape[0])
            fours = jnp.maximum(last - first, 0) >> 2
            lax.fori_loop(0, fours, four, 0)
            lax.fori_loop(first + 4 * fours, last, body, 0)


def place(origins, order, counts, where, pieces, shape, base=None):
    bases = [] if base is None else [base]
    slots = sum(piece.shape[0] for piece in pieces)
    return pl.pallas_call(
        functools.partial(place_kernel, origins),
        out_shape=jax.ShapeDtypeStruct(shape, pieces[0].dtype),
        in_specs=[SMEM] * 3 + [VMEM] * len(pieces) + [HBM] * len(bases),
        out_specs=HBM,
        input_output_aliases={3 + len(pieces): 0} if bases else {},
        scratch_shapes=[
            pltpu.VMEM((slots,) + shape[1:], pieces[0].dtype),
            pltpu.SemaphoreType.DMA((shape[0],)),
        ],
        compiler_params=pltpu.CompilerParams(vmem_limit_bytes=16 * 2**20),
        name="place_blocks",
    )(order, counts, where, *pieces, *bases)


def spread(slots, shape, seats, order, counts, where, blocks):
    split = (slots + 1) // 2
    own = select(seats, order, counts, where, blocks, slots)
    low, high = own[:split], own[split:]
    below_low, above_high = hop_y(low, 1), hop_y(high, -1)
    below_high, above_low = hop_y(high, 1), hop_y(low, -1)
    far = [hop_y(below_low, 1), hop_y(above_high, -1)]
    early = lax.optimization_barrier([own, below_low, above_high])
    early += [hop_core(piece) for piece in early]
    origins = [(core, *origin) for core in range(NC) for origin in ((0, 0), (3, 0), (1, split))]
    updates = place(origins, order, counts, where, early, shape)
    late = lax.optimization_barrier([below_high, above_low] + far)
    late += [hop_core(piece) for piece in late]
    origins = [(core, *origin) for core in range(NC) for origin in ((3, split), (1, 0), (2, 0), (2, split))]
    return place(origins, order, counts, where, late, shape, updates)


def on_device(grads, momentum, owners):
    count = owners.shape[0]
    group = lax.axis_index("dp")
    me = lax.axis_index(AXES)
    where = group[None].astype(jnp.int32)
    packed = pack(owners, where, grads)
    rows = lax.all_to_all(packed, AXES, 0, 0, tiled=True, axis_index_groups=MEMBERS)

    ids = jnp.arange(count, dtype=jnp.int32)
    homes = owners // SHARDS
    seats = seat((owners >> 2) & (NZ - 1), owners & (NX - 1))
    before = (homes[:, None] == homes[None, :]) & (owners[None, :] < owners[:, None])
    slot = homes * SHARDS + jnp.sum(before.astype(jnp.int32), axis=1)
    order = jnp.sum(
        jnp.where(slot[None, :] == jnp.arange(GROUPS * SHARDS, dtype=jnp.int32)[:, None], ids[None, :], 0), axis=1
    )
    counts = jnp.sum((homes[None, :] == jnp.arange(GROUPS, dtype=jnp.int32)[:, None]).astype(jnp.int32), axis=1)
    owned = jnp.any(owners == me)[None].astype(jnp.int32)

    blocks, following = muon_step(owned, rows, momentum[0].T)
    blocks = lax.all_to_all(blocks, AXES, 0, 0, tiled=True, axis_index_groups=MEMBERS)
    few = 19
    updates = lax.cond(
        jnp.max(counts) <= few,
        functools.partial(spread, few, grads.shape),
        functools.partial(spread, SHARDS, grads.shape),
        seats,
        order,
        counts,
        where,
        blocks,
    )
    return (updates, following.T[None])


def solution(mesh):
    return jax.shard_map(
        on_device,
        mesh=mesh,
        in_specs=(P(None, "shard", None), P(AXES, None, None), P()),
        out_specs=(P(None, "shard", None), P(AXES, None, None)),
        check_vma=False,
    )
```

```python
import functools
import math

import jax
import jax.numpy as jnp
from jax import lax
from jax.experimental import pallas as pl
from jax.experimental.pallas import tpu as pltpu
from jax.sharding import PartitionSpec as P

DECAY = 0.95
LINEAR, CUBIC, QUINTIC = 3.4445, -4.775, 2.0315
EPS = 1e-07
ITERS = 2
AXES = ("dp", "shard")
NZ, NX, NC, NY = 8, 4, 2, 4
SHARDS = NZ * NX
GROUPS = NY * NC
NT = (((1,), (1,)), ((), ()))
NN = (((1,), (0,)), ((), ()))
ANY = pl.BlockSpec(memory_space=pl.ANY)
HBM = pl.BlockSpec(memory_space=pltpu.HBM)
SMEM = pl.BlockSpec(memory_space=pltpu.SMEM)
VMEM = pl.BlockSpec(memory_space=pltpu.VMEM)


def seat(z, x):
    pick = jnp.where if isinstance(z, jax.Array) else (lambda c, a, b: a if c else b)
    return pick(z < NZ // 2, 2 * z, 2 * NZ - 1 - 2 * z) + NZ * pick(x < NX // 2, 2 * x, 2 * NX - 1 - 2 * x)


SEATED = sorted(range(SHARDS), key=lambda s: seat(s // NX, s % NX))
MEMBERS = [[g * SHARDS + s for s in SEATED] for g in range(GROUPS)]


def hop_y(array, step):
    count, along = GROUPS * SHARDS, NC * SHARDS
    return lax.ppermute(array, AXES, [(d, (d + along * step) % count) for d in range(count)])


def hop_core(array):
    return lax.ppermute(array, AXES, [(d, d ^ SHARDS) for d in range(GROUPS * SHARDS)])


LANES = 128


def put_dense(out, index, block):
    n, columns = block.shape
    whole = columns // LANES
    for tile in range(whole):
        out[index, tile * n : (tile + 1) * n] = block[:, tile * LANES : (tile + 1) * LANES]
    rest = block[:, whole * LANES :]
    out[index, whole * n :] = jnp.concatenate([rest[: n // 2], rest[n // 2 :]], axis=1)


def get_dense(blocks, index, n):
    whole = blocks.shape[1] // n
    tiles = [blocks[index, tile * n : (tile + 1) * n] for tile in range(whole)]
    rest = blocks[index, whole * n :]
    return tiles + [jnp.concatenate([rest[:, : LANES // 2], rest[:, LANES // 2 :]], axis=0)]


def dense_rows(n, columns):
    return n * columns // LANES


def pack_kernel(owners, group, grads, out, rows, dense, places, sems, back):
    count, unroll = owners.shape[0], 8

    def copy(m, k):
        return pltpu.make_async_copy(grads.at[m], rows.at[k], sems.at[k])

    def look(m, found):
        owner = owners[m]
        mine = (owner >> 5) == group[0]

        @pl.when(mine)
        def _():
            copy(m, found).start()
            places[found] = seat((owner >> 2) & (NZ - 1), owner & (NX - 1))

        return found + mine.astype(jnp.int32)

    def look_many(i, found):
        for j in range(unroll):
            found = look(i * unroll + j, found)
        return found

    found = lax.fori_loop(0, count // unroll, look_many, jnp.int32(0))
    for m in range(count // unroll * unroll, count):
        found = look(m, found)

    def send(k):
        return pltpu.make_async_copy(dense.at[k], out.at[places[k]], back.at[k])

    def store(k, carry):
        copy(0, k).wait()
        put_dense(dense, k, rows[k])
        send(k).start()
        return carry

    def finish(k, carry):
        send(k).wait()
        return carry

    lax.fori_loop(0, found, store, 0)
    lax.fori_loop(0, found, finish, 0)


def pack(owners, group, grads):
    _, rows, columns = grads.shape
    return pl.pallas_call(
        pack_kernel,
        out_shape=jax.ShapeDtypeStruct((SHARDS, dense_rows(rows, columns), LANES), grads.dtype),
        in_specs=[SMEM, SMEM, HBM],
        out_specs=HBM,
        scratch_shapes=[
            pltpu.VMEM((SHARDS, rows, columns), grads.dtype),
            pltpu.VMEM((SHARDS, dense_rows(rows, columns), LANES), grads.dtype),
            pltpu.SMEM((SHARDS,), jnp.int32),
            pltpu.SemaphoreType.DMA((SHARDS,)),
            pltpu.SemaphoreType.DMA((SHARDS,)),
        ],
        compiler_params=pltpu.CompilerParams(vmem_limit_bytes=56 * 2**20),
        name="pack_rows",
    )(owners, group, grads)


def dot(a, b, dims):
    return lax.dot_general(a, b, dims, preferred_element_type=jnp.float32)


def step_kernel(scale, owned_ref, rows_ref, mom_ref, out_ref, next_hbm, blend, cur, gram, poly, next_ref, sem):
    rows = mom_ref.shape[1] // SHARDS
    span = NX * rows
    owned = owned_ref[0] > 0
    total = jnp.zeros((8, span), jnp.float32)
    for z in range(NZ):
        cols = slice(z * span, (z + 1) * span)
        tiles = zip(*[get_dense(rows_ref, seat(z, x), rows) for x in range(NX)])
        grad = jnp.concatenate([jnp.concatenate(tile, axis=0) for tile in tiles], axis=1)
        grad = jnp.where(owned, grad.T.astype(jnp.float32), 0.0)
        renewed = DECAY * mom_ref[:, cols].astype(jnp.float32) + grad
        next_ref[:, cols] = renewed.astype(jnp.bfloat16)
        mixed = grad + DECAY * renewed
        blend[:, cols] = mixed
        total = total + jnp.sum((mixed * mixed).reshape(-1, 8, span), axis=0)
    keep = pltpu.make_async_copy(next_ref, next_hbm, sem)
    keep.start()
    inverse = 1.0 / (jnp.sqrt(jnp.sum(total)) + EPS)
    cur[...] = (blend[...] * inverse).astype(jnp.bfloat16)
    columns, total_rows = cur.shape
    cuts = [(low, min(low + 256, columns)) for low in range(0, columns, 256)]
    wide = 2 * span
    for iteration in range(ITERS):
        for low, high in cuts:
            block = dot(cur[:high], cur[low:high], NT).astype(jnp.bfloat16)
            gram[:high, low:high] = block
            if low:
                gram[low:high, :low] = block[:low].T
        for low, high in cuts:
            square = dot(gram[:high], gram[:, low:high], NN)
            block = (CUBIC * gram[:high, low:high].astype(jnp.float32) + QUINTIC * square).astype(jnp.bfloat16)
            poly[:high, low:high] = block
            if low:
                poly[low:high, :low] = block[:low].T
        factor = poly[...]
        if iteration + 1 < ITERS:
            x = cur[...]
            cur[...] = (LINEAR * x.astype(jnp.float32) + dot(factor, x, NN)).astype(jnp.bfloat16)
            continue
        for left in range(0, total_rows, wide):
            x = cur[:, left : left + wide]
            last = (scale * LINEAR) * x.astype(jnp.float32) + scale * dot(factor, x, NN)
            last = last.astype(jnp.bfloat16)
            for z in range(left // span, (left + wide) // span):
                update = last[:, z * span - left : (z + 1) * span - left].T
                for x in range(NX):
                    put_dense(out_ref, seat(z, x), update[x * rows : (x + 1) * rows])
    keep.wait()


def muon_step(owned, rows, momentum_t):
    columns, total_rows = momentum_t.shape
    scale = 0.2 * math.sqrt(max(columns, total_rows))
    square = pltpu.VMEM((columns, columns), jnp.bfloat16)
    return pl.pallas_call(
        functools.partial(step_kernel, scale),
        out_shape=(
            jax.ShapeDtypeStruct(rows.shape, jnp.bfloat16),
            jax.ShapeDtypeStruct(momentum_t.shape, jnp.bfloat16),
        ),
        in_specs=[SMEM, VMEM, VMEM],
        out_specs=(VMEM, HBM),
        scratch_shapes=[
            pltpu.VMEM(momentum_t.shape, jnp.float32),
            pltpu.VMEM(momentum_t.shape, jnp.bfloat16),
            square,
            square,
            pltpu.VMEM(momentum_t.shape, jnp.bfloat16),
            pltpu.SemaphoreType.DMA,
        ],
        compiler_params=pltpu.CompilerParams(vmem_limit_bytes=24 * 2**20),
        name="newton_schulz",
    )(owned, rows, momentum_t)


def select_kernel(seats, order, counts, where, blocks, out):
    group = where[0]

    def body(k, carry):
        out[k] = blocks[seats[order[group * SHARDS + k]]]
        return carry

    lax.fori_loop(0, counts[group], body, 0)


def select(seats, order, counts, where, blocks, slots):
    return pl.pallas_call(
        select_kernel,
        out_shape=jax.ShapeDtypeStruct((slots,) + blocks.shape[1:], blocks.dtype),
        in_specs=[SMEM] * 4 + [VMEM],
        out_specs=VMEM,
        compiler_params=pltpu.CompilerParams(vmem_limit_bytes=16 * 2**20),
        name="select_blocks",
    )(seats, order, counts, where, blocks)


def place_kernel(origins, order, counts, where, *refs):
    pieces, (out, rows, sems) = refs[: len(origins)], refs[-3:]
    height = out.shape[1]
    offsets = [sum(piece.shape[0] for piece in pieces[:i]) for i in range(len(pieces))]

    def unpack(chosen, k, carry):
        for i in chosen:
            for tile, value in enumerate(get_dense(pieces[i], k, height)):
                left = tile * LANES
                rows[offsets[i] + k, :, left : left + value.shape[1]] = value
        return carry

    homes = [((where[0] ^ core) + NC * hop) & (GROUPS - 1) for core, hop, _ in origins]

    def copy(i, k):
        m = order[homes[i] * SHARDS + origins[i][2] + k]
        return pltpu.make_async_copy(rows.at[offsets[i] + k], out.at[m], sems.at[m])

    def start(chosen, k, carry):
        unpack(chosen, k, carry)
        for i in chosen:
            pl.when(origins[i][2] + k < counts[homes[i]])(lambda i=i: copy(i, k).start())
        return carry

    done = 0
    for size in sorted({piece.shape[0] for piece in pieces}):
        chosen = [i for i, piece in enumerate(pieces) if piece.shape[0] >= size]
        lax.fori_loop(done, size, functools.partial(start, chosen), 0)
        done = size

    for i, piece in enumerate(pieces):

        def wait(k, carry, i=i):
            copy(i, k).wait()
            return carry

        lax.fori_loop(0, jnp.minimum(counts[homes[i]] - origins[i][2], piece.shape[0]), wait, 0)


def place(origins, order, counts, where, pieces, shape, base=None):
    bases = [] if base is None else [base]
    slots = sum(piece.shape[0] for piece in pieces)
    return pl.pallas_call(
        functools.partial(place_kernel, origins),
        out_shape=jax.ShapeDtypeStruct(shape, pieces[0].dtype),
        in_specs=[SMEM] * 3 + [VMEM] * len(pieces) + [HBM] * len(bases),
        out_specs=HBM,
        input_output_aliases={3 + len(pieces): 0} if bases else {},
        scratch_shapes=[
            pltpu.VMEM((slots,) + shape[1:], pieces[0].dtype),
            pltpu.SemaphoreType.DMA((shape[0],)),
        ],
        compiler_params=pltpu.CompilerParams(vmem_limit_bytes=16 * 2**20),
        name="place_blocks",
    )(order, counts, where, *pieces, *bases)


def spread(slots, shape, seats, order, counts, where, blocks):
    split = (slots + 1) // 2
    own = select(seats, order, counts, where, blocks, slots)
    low, high = own[:split], own[split:]
    below_low, above_high = hop_y(low, 1), hop_y(high, -1)
    below_high, above_low = hop_y(high, 1), hop_y(low, -1)
    far = [hop_y(below_low, 1), hop_y(above_high, -1)]
    early = lax.optimization_barrier([own, below_low, above_high])
    early += [hop_core(piece) for piece in early]
    origins = [(core, *origin) for core in range(NC) for origin in ((0, 0), (3, 0), (1, split))]
    updates = place(origins, order, counts, where, early, shape)
    late = lax.optimization_barrier([below_high, above_low] + far)
    late += [hop_core(piece) for piece in late]
    origins = [(core, *origin) for core in range(NC) for origin in ((3, split), (1, 0), (2, 0), (2, split))]
    return place(origins, order, counts, where, late, shape, updates)


def on_device(grads, momentum, owners):
    count = owners.shape[0]
    group = lax.axis_index("dp")
    me = lax.axis_index(AXES)
    where = group[None].astype(jnp.int32)
    packed = pack(owners, where, grads)
    rows = lax.all_to_all(packed, AXES, 0, 0, tiled=True, axis_index_groups=MEMBERS)

    ids = jnp.arange(count, dtype=jnp.int32)
    homes = owners // SHARDS
    seats = seat((owners >> 2) & (NZ - 1), owners & (NX - 1))
    before = (homes[:, None] == homes[None, :]) & (owners[None, :] < owners[:, None])
    slot = homes * SHARDS + jnp.sum(before.astype(jnp.int32), axis=1)
    order = jnp.sum(
        jnp.where(slot[None, :] == jnp.arange(GROUPS * SHARDS, dtype=jnp.int32)[:, None], ids[None, :], 0), axis=1
    )
    counts = jnp.sum((homes[None, :] == jnp.arange(GROUPS, dtype=jnp.int32)[:, None]).astype(jnp.int32), axis=1)
    owned = jnp.any(owners == me)[None].astype(jnp.int32)

    blocks, following = muon_step(owned, rows, momentum[0].T)
    blocks = lax.all_to_all(blocks, AXES, 0, 0, tiled=True, axis_index_groups=MEMBERS)
    few = 19
    updates = lax.cond(
        jnp.max(counts) <= few,
        functools.partial(spread, few, grads.shape),
        functools.partial(spread, SHARDS, grads.shape),
        seats,
        order,
        counts,
        where,
        blocks,
    )
    return (updates, following.T[None])


def solution(mesh):
    return jax.shard_map(
        on_device,
        mesh=mesh,
        in_specs=(P(None, "shard", None), P(AXES, None, None), P()),
        out_specs=(P(None, "shard", None), P(AXES, None, None)),
        check_vma=False,
    )
```

```python
import functools
import math

import jax
import jax.numpy as jnp
from jax import lax
from jax.experimental import pallas as pl
from jax.experimental.pallas import tpu as pltpu
from jax.sharding import PartitionSpec as P

DECAY = 0.95
LINEAR, CUBIC, QUINTIC = 3.4445, -4.775, 2.0315
EPS = 1e-07
ITERS = 2
AXES = ("dp", "shard")
NZ, NX, NC, NY = 8, 4, 2, 4
SHARDS = NZ * NX
GROUPS = NY * NC
NT = (((1,), (1,)), ((), ()))
NN = (((1,), (0,)), ((), ()))
ANY = pl.BlockSpec(memory_space=pl.ANY)
HBM = pl.BlockSpec(memory_space=pltpu.HBM)
SMEM = pl.BlockSpec(memory_space=pltpu.SMEM)
VMEM = pl.BlockSpec(memory_space=pltpu.VMEM)


def seat(z, x):
    pick = jnp.where if isinstance(z, jax.Array) else (lambda c, a, b: a if c else b)
    return pick(z < NZ // 2, 2 * z, 2 * NZ - 1 - 2 * z) + NZ * pick(x < NX // 2, 2 * x, 2 * NX - 1 - 2 * x)


SEATED = sorted(range(SHARDS), key=lambda s: seat(s // NX, s % NX))
MEMBERS = [[g * SHARDS + s for s in SEATED] for g in range(GROUPS)]


def hop_y(array, step):
    count, along = GROUPS * SHARDS, NC * SHARDS
    return lax.ppermute(array, AXES, [(d, (d + along * step) % count) for d in range(count)])


def hop_core(array):
    return lax.ppermute(array, AXES, [(d, d ^ SHARDS) for d in range(GROUPS * SHARDS)])


LANES = 128


def put_dense(out, index, block):
    n, columns = block.shape
    whole = columns // LANES
    for tile in range(whole):
        out[index, tile * n : (tile + 1) * n] = block[:, tile * LANES : (tile + 1) * LANES]
    rest = block[:, whole * LANES :]
    out[index, whole * n :] = jnp.concatenate([rest[: n // 2], rest[n // 2 :]], axis=1)


def get_dense(blocks, index, n):
    whole = blocks.shape[1] // n
    tiles = [blocks[index, tile * n : (tile + 1) * n] for tile in range(whole)]
    rest = blocks[index, whole * n :]
    return tiles + [jnp.concatenate([rest[:, : LANES // 2], rest[:, LANES // 2 :]], axis=0)]


def dense_rows(n, columns):
    return n * columns // LANES


def pack_kernel(owners, group, grads, out, rows, dense, places, sems, back):
    count, unroll = owners.shape[0], 8

    def copy(m, k):
        return pltpu.make_async_copy(grads.at[m], rows.at[k], sems.at[k])

    def look(m, found):
        owner = owners[m]
        mine = (owner >> 5) == group[0]

        @pl.when(mine)
        def _():
            copy(m, found).start()
            places[found] = seat((owner >> 2) & (NZ - 1), owner & (NX - 1))

        return found + mine.astype(jnp.int32)

    def look_many(i, found):
        for j in range(unroll):
            found = look(i * unroll + j, found)
        return found

    found = lax.fori_loop(0, count // unroll, look_many, jnp.int32(0))
    for m in range(count // unroll * unroll, count):
        found = look(m, found)

    def send(k):
        return pltpu.make_async_copy(dense.at[k], out.at[places[k]], back.at[k])

    def store(k, carry):
        copy(0, k).wait()
        put_dense(dense, k, rows[k])
        send(k).start()
        return carry

    def finish(k, carry):
        send(k).wait()
        return carry

    lax.fori_loop(0, found, store, 0)
    lax.fori_loop(0, found, finish, 0)


def pack(owners, group, grads):
    _, rows, columns = grads.shape
    return pl.pallas_call(
        pack_kernel,
        out_shape=jax.ShapeDtypeStruct((SHARDS, dense_rows(rows, columns), LANES), grads.dtype),
        in_specs=[SMEM, SMEM, HBM],
        out_specs=HBM,
        scratch_shapes=[
            pltpu.VMEM((SHARDS, rows, columns), grads.dtype),
            pltpu.VMEM((SHARDS, dense_rows(rows, columns), LANES), grads.dtype),
            pltpu.SMEM((SHARDS,), jnp.int32),
            pltpu.SemaphoreType.DMA((SHARDS,)),
            pltpu.SemaphoreType.DMA((SHARDS,)),
        ],
        compiler_params=pltpu.CompilerParams(vmem_limit_bytes=56 * 2**20),
        name="pack_rows",
    )(owners, group, grads)


def dot(a, b, dims):
    return lax.dot_general(a, b, dims, preferred_element_type=jnp.float32)


def step_kernel(scale, owned_ref, rows_ref, mom_ref, out_ref, next_hbm, blend, cur, gram, poly, next_ref, sem):
    rows = mom_ref.shape[1] // SHARDS
    span = NX * rows
    owned = owned_ref[0] > 0
    total = jnp.zeros((8, span), jnp.float32)
    for z in range(NZ):
        cols = slice(z * span, (z + 1) * span)
        tiles = zip(*[get_dense(rows_ref, seat(z, x), rows) for x in range(NX)])
        grad = jnp.concatenate([jnp.concatenate(tile, axis=0) for tile in tiles], axis=1)
        grad = jnp.where(owned, grad.T.astype(jnp.float32), 0.0)
        renewed = DECAY * mom_ref[:, cols].astype(jnp.float32) + grad
        next_ref[:, cols] = renewed.astype(jnp.bfloat16)
        mixed = grad + DECAY * renewed
        blend[:, cols] = mixed
        total = total + jnp.sum((mixed * mixed).reshape(-1, 8, span), axis=0)
    keep = pltpu.make_async_copy(next_ref, next_hbm, sem)
    keep.start()
    inverse = 1.0 / (jnp.sqrt(jnp.sum(total)) + EPS)
    cur[...] = (blend[...] * inverse).astype(jnp.bfloat16)
    columns, total_rows = cur.shape
    cuts = [(low, min(low + 256, columns)) for low in range(0, columns, 256)]
    wide = 2 * span
    for iteration in range(ITERS):
        for low, high in cuts:
            block = dot(cur[:high], cur[low:high], NT).astype(jnp.bfloat16)
            gram[:high, low:high] = block
            if low:
                gram[low:high, :low] = block[:low].T
        for low, high in cuts:
            square = dot(gram[:high], gram[:, low:high], NN)
            block = (CUBIC * gram[:high, low:high].astype(jnp.float32) + QUINTIC * square).astype(jnp.bfloat16)
            poly[:high, low:high] = block
            if low:
                poly[low:high, :low] = block[:low].T
        factor = poly[...]
        if iteration + 1 < ITERS:
            x = cur[...]
            cur[...] = (LINEAR * x.astype(jnp.float32) + dot(factor, x, NN)).astype(jnp.bfloat16)
            continue
        for left in range(0, total_rows, wide):
            x = cur[:, left : left + wide]
            last = (scale * LINEAR) * x.astype(jnp.float32) + scale * dot(factor, x, NN)
            last = last.astype(jnp.bfloat16)
            for z in range(left // span, (left + wide) // span):
                update = last[:, z * span - left : (z + 1) * span - left].T
                for x in range(NX):
                    put_dense(out_ref, seat(z, x), update[x * rows : (x + 1) * rows])
    keep.wait()


def muon_step(owned, rows, momentum_t):
    columns, total_rows = momentum_t.shape
    scale = 0.2 * math.sqrt(max(columns, total_rows))
    square = pltpu.VMEM((columns, columns), jnp.bfloat16)
    return pl.pallas_call(
        functools.partial(step_kernel, scale),
        out_shape=(
            jax.ShapeDtypeStruct(rows.shape, jnp.bfloat16),
            jax.ShapeDtypeStruct(momentum_t.shape, jnp.bfloat16),
        ),
        in_specs=[SMEM, VMEM, VMEM],
        out_specs=(VMEM, HBM),
        scratch_shapes=[
            pltpu.VMEM(momentum_t.shape, jnp.float32),
            pltpu.VMEM(momentum_t.shape, jnp.bfloat16),
            square,
            square,
            pltpu.VMEM(momentum_t.shape, jnp.bfloat16),
            pltpu.SemaphoreType.DMA,
        ],
        compiler_params=pltpu.CompilerParams(vmem_limit_bytes=24 * 2**20),
        name="newton_schulz",
    )(owned, rows, momentum_t)


def select_kernel(seats, order, counts, where, blocks, out):
    group = where[0]

    def body(k, carry):
        out[k] = blocks[seats[order[group * SHARDS + k]]]
        return carry

    lax.fori_loop(0, counts[group], body, 0)


def select(seats, order, counts, where, blocks, slots):
    return pl.pallas_call(
        select_kernel,
        out_shape=jax.ShapeDtypeStruct((slots,) + blocks.shape[1:], blocks.dtype),
        in_specs=[SMEM] * 4 + [VMEM],
        out_specs=VMEM,
        compiler_params=pltpu.CompilerParams(vmem_limit_bytes=16 * 2**20),
        name="select_blocks",
    )(seats, order, counts, where, blocks)


def place_kernel(origins, order, counts, where, *refs):
    pieces, (out, rows, sems) = refs[: len(origins)], refs[-3:]
    height = out.shape[1]
    offsets = [sum(piece.shape[0] for piece in pieces[:i]) for i in range(len(pieces))]

    def unpack(chosen, k, carry):
        for i in chosen:
            for tile, value in enumerate(get_dense(pieces[i], k, height)):
                left = tile * LANES
                rows[offsets[i] + k, :, left : left + value.shape[1]] = value
        return carry

    homes = [((where[0] ^ core) + NC * hop) & (GROUPS - 1) for core, hop, _ in origins]

    def copy(i, k):
        m = order[homes[i] * SHARDS + origins[i][2] + k]
        return pltpu.make_async_copy(rows.at[offsets[i] + k], out.at[m], sems.at[m])

    def start(chosen, k, carry):
        unpack(chosen, k, carry)
        for i in chosen:
            pl.when(origins[i][2] + k < counts[homes[i]])(lambda i=i: copy(i, k).start())
        return carry

    done = 0
    for size in sorted({piece.shape[0] for piece in pieces}):
        chosen = [i for i, piece in enumerate(pieces) if piece.shape[0] >= size]
        lax.fori_loop(done, size, functools.partial(start, chosen), 0)
        done = size

    for i, piece in enumerate(pieces):

        def wait(k, carry, i=i):
            copy(i, k).wait()
            return carry

        lax.fori_loop(0, jnp.minimum(counts[homes[i]] - origins[i][2], piece.shape[0]), wait, 0)


def place(origins, order, counts, where, pieces, shape, base=None):
    bases = [] if base is None else [base]
    slots = sum(piece.shape[0] for piece in pieces)
    return pl.pallas_call(
        functools.partial(place_kernel, origins),
        out_shape=jax.ShapeDtypeStruct(shape, pieces[0].dtype),
        in_specs=[SMEM] * 3 + [VMEM] * len(pieces) + [HBM] * len(bases),
        out_specs=HBM,
        input_output_aliases={3 + len(pieces): 0} if bases else {},
        scratch_shapes=[
            pltpu.VMEM((slots,) + shape[1:], pieces[0].dtype),
            pltpu.SemaphoreType.DMA((shape[0],)),
        ],
        compiler_params=pltpu.CompilerParams(vmem_limit_bytes=16 * 2**20),
        name="place_blocks",
    )(order, counts, where, *pieces, *bases)


def spread(slots, shape, seats, order, counts, where, blocks):
    split = (slots + 1) // 2
    own = select(seats, order, counts, where, blocks, slots)
    low, high = own[:split], own[split:]
    below_low, above_high = hop_y(low, 1), hop_y(high, -1)
    below_high, above_low = hop_y(high, 1), hop_y(low, -1)
    far = [hop_y(below_low, 1), hop_y(above_high, -1)]
    def at(core, origins):
        return [(core, *origin) for origin in origins]

    tables = (order, counts, where)
    early = lax.optimization_barrier([own, below_low, above_high])
    early_origins = [(0, 0), (3, 0), (1, split)]
    late_origins = [(3, split), (1, 0), (2, 0), (2, split)]
    updates = place(at(0, early_origins), *tables, early, shape)
    updates, *late = lax.optimization_barrier([updates, below_high, above_low] + far)
    early_other = [hop_core(piece) for piece in early]
    late_other = [hop_core(piece) for piece in late]
    origins = at(1, early_origins) + at(0, late_origins)
    updates = place(origins, *tables, early_other + late, shape, updates)
    return place(at(1, late_origins), *tables, late_other, shape, updates)


def on_device(grads, momentum, owners):
    count = owners.shape[0]
    group = lax.axis_index("dp")
    me = lax.axis_index(AXES)
    where = group[None].astype(jnp.int32)
    packed = pack(owners, where, grads)
    rows = lax.all_to_all(packed, AXES, 0, 0, tiled=True, axis_index_groups=MEMBERS)

    ids = jnp.arange(count, dtype=jnp.int32)
    homes = owners // SHARDS
    seats = seat((owners >> 2) & (NZ - 1), owners & (NX - 1))
    before = (homes[:, None] == homes[None, :]) & (owners[None, :] < owners[:, None])
    slot = homes * SHARDS + jnp.sum(before.astype(jnp.int32), axis=1)
    order = jnp.sum(
        jnp.where(slot[None, :] == jnp.arange(GROUPS * SHARDS, dtype=jnp.int32)[:, None], ids[None, :], 0), axis=1
    )
    counts = jnp.sum((homes[None, :] == jnp.arange(GROUPS, dtype=jnp.int32)[:, None]).astype(jnp.int32), axis=1)
    owned = jnp.any(owners == me)[None].astype(jnp.int32)

    blocks, following = muon_step(owned, rows, momentum[0].T)
    blocks = lax.all_to_all(blocks, AXES, 0, 0, tiled=True, axis_index_groups=MEMBERS)
    few = 19
    updates = lax.cond(
        jnp.max(counts) <= few,
        functools.partial(spread, few, grads.shape),
        functools.partial(spread, SHARDS, grads.shape),
        seats,
        order,
        counts,
        where,
        blocks,
    )
    return (updates, following.T[None])


def solution(mesh):
    return jax.shard_map(
        on_device,
        mesh=mesh,
        in_specs=(P(None, "shard", None), P(AXES, None, None), P()),
        out_specs=(P(None, "shard", None), P(AXES, None, None)),
        check_vma=False,
    )
```

```python
import functools
import math

import jax
import jax.numpy as jnp
from jax import lax
from jax.experimental import pallas as pl
from jax.experimental.pallas import tpu as pltpu
from jax.sharding import PartitionSpec as P

DECAY = 0.95
LINEAR, CUBIC, QUINTIC = 3.4445, -4.775, 2.0315
EPS = 1e-07
ITERS = 2
AXES = ("dp", "shard")
NZ, NX, NC, NY = 8, 4, 2, 4
SHARDS = NZ * NX
GROUPS = NY * NC
NT = (((1,), (1,)), ((), ()))
NN = (((1,), (0,)), ((), ()))
ANY = pl.BlockSpec(memory_space=pl.ANY)
HBM = pl.BlockSpec(memory_space=pltpu.HBM)
SMEM = pl.BlockSpec(memory_space=pltpu.SMEM)
VMEM = pl.BlockSpec(memory_space=pltpu.VMEM)


def seat(z, x):
    pick = jnp.where if isinstance(z, jax.Array) else (lambda c, a, b: a if c else b)
    return NX * pick(z < NZ // 2, 2 * z, 2 * NZ - 1 - 2 * z) + pick(x < NX // 2, 2 * x, 2 * NX - 1 - 2 * x)


SEATED = sorted(range(SHARDS), key=lambda s: seat(s // NX, s % NX))
MEMBERS = [[g * SHARDS + s for s in SEATED] for g in range(GROUPS)]


def hop_y(array, step):
    count, along = GROUPS * SHARDS, NC * SHARDS
    return lax.ppermute(array, AXES, [(d, (d + along * step) % count) for d in range(count)])


def hop_core(array):
    return lax.ppermute(array, AXES, [(d, d ^ SHARDS) for d in range(GROUPS * SHARDS)])


LANES = 128


def put_dense(out, index, block):
    n, columns = block.shape
    whole = columns // LANES
    for tile in range(whole):
        out[index, tile * n : (tile + 1) * n] = block[:, tile * LANES : (tile + 1) * LANES]
    rest = block[:, whole * LANES :]
    out[index, whole * n :] = jnp.concatenate([rest[: n // 2], rest[n // 2 :]], axis=1)


def get_dense(blocks, index, n):
    whole = blocks.shape[1] // n
    tiles = [blocks[index, tile * n : (tile + 1) * n] for tile in range(whole)]
    rest = blocks[index, whole * n :]
    return tiles + [jnp.concatenate([rest[:, : LANES // 2], rest[:, LANES // 2 :]], axis=0)]


def dense_rows(n, columns):
    return n * columns // LANES


def pack_kernel(owners, group, grads, out, rows, dense, places, sems, back):
    count, unroll = owners.shape[0], 8

    def copy(m, k):
        return pltpu.make_async_copy(grads.at[m], rows.at[k], sems.at[k])

    def look(m, found):
        owner = owners[m]
        mine = (owner >> 5) == group[0]

        @pl.when(mine)
        def _():
            copy(m, found).start()
            places[found] = seat((owner >> 2) & (NZ - 1), owner & (NX - 1))

        return found + mine.astype(jnp.int32)

    def look_many(i, found):
        for j in range(unroll):
            found = look(i * unroll + j, found)
        return found

    found = lax.fori_loop(0, count // unroll, look_many, jnp.int32(0))
    for m in range(count // unroll * unroll, count):
        found = look(m, found)

    def send(k):
        return pltpu.make_async_copy(dense.at[k], out.at[places[k]], back.at[k])

    def store(k, carry):
        copy(0, k).wait()
        put_dense(dense, k, rows[k])
        send(k).start()
        return carry

    def finish(k, carry):
        send(k).wait()
        return carry

    lax.fori_loop(0, found, store, 0)
    lax.fori_loop(0, found, finish, 0)


def pack(owners, group, grads):
    _, rows, columns = grads.shape
    return pl.pallas_call(
        pack_kernel,
        out_shape=jax.ShapeDtypeStruct((SHARDS, dense_rows(rows, columns), LANES), grads.dtype),
        in_specs=[SMEM, SMEM, HBM],
        out_specs=HBM,
        scratch_shapes=[
            pltpu.VMEM((SHARDS, rows, columns), grads.dtype),
            pltpu.VMEM((SHARDS, dense_rows(rows, columns), LANES), grads.dtype),
            pltpu.SMEM((SHARDS,), jnp.int32),
            pltpu.SemaphoreType.DMA((SHARDS,)),
            pltpu.SemaphoreType.DMA((SHARDS,)),
        ],
        compiler_params=pltpu.CompilerParams(vmem_limit_bytes=56 * 2**20),
        name="pack_rows",
    )(owners, group, grads)


def dot(a, b, dims):
    return lax.dot_general(a, b, dims, preferred_element_type=jnp.float32)


def step_kernel(scale, owned_ref, rows_ref, mom_ref, out_hbm, next_hbm, blend, cur, gram, poly, next_ref, out_ref, sem, sems):
    rows = mom_ref.shape[1] // SHARDS
    span = NX * rows
    owned = owned_ref[0] > 0
    total = jnp.zeros((8, span), jnp.float32)
    for z in range(NZ):
        cols = slice(z * span, (z + 1) * span)
        tiles = zip(*[get_dense(rows_ref, seat(z, x), rows) for x in range(NX)])
        grad = jnp.concatenate([jnp.concatenate(tile, axis=0) for tile in tiles], axis=1)
        grad = jnp.where(owned, grad.T.astype(jnp.float32), 0.0)
        renewed = DECAY * mom_ref[:, cols].astype(jnp.float32) + grad
        next_ref[:, cols] = renewed.astype(jnp.bfloat16)
        mixed = grad + DECAY * renewed
        blend[:, cols] = mixed
        total = total + jnp.sum((mixed * mixed).reshape(-1, 8, span), axis=0)
    keep = pltpu.make_async_copy(next_ref, next_hbm, sem)
    keep.start()
    sent = []
    inverse = 1.0 / (jnp.sqrt(jnp.sum(total)) + EPS)
    cur[...] = (blend[...] * inverse).astype(jnp.bfloat16)
    columns, total_rows = cur.shape
    cuts = [(low, min(low + 256, columns)) for low in range(0, columns, 256)]
    wide = 2 * span
    for iteration in range(ITERS):
        for low, high in cuts:
            block = dot(cur[:high], cur[low:high], NT).astype(jnp.bfloat16)
            gram[:high, low:high] = block
            if low:
                gram[low:high, :low] = block[:low].T
        for low, high in cuts:
            square = dot(gram[:high], gram[:, low:high], NN)
            block = (CUBIC * gram[:high, low:high].astype(jnp.float32) + QUINTIC * square).astype(jnp.bfloat16)
            poly[:high, low:high] = block
            if low:
                poly[low:high, :low] = block[:low].T
        factor = poly[...]
        if iteration + 1 < ITERS:
            x = cur[...]
            cur[...] = (LINEAR * x.astype(jnp.float32) + dot(factor, x, NN)).astype(jnp.bfloat16)
            continue
        for left in range(0, total_rows, wide):
            x = cur[:, left : left + wide]
            last = (scale * LINEAR) * x.astype(jnp.float32) + scale * dot(factor, x, NN)
            last = last.astype(jnp.bfloat16)
            for z in range(left // span, (left + wide) // span):
                update = last[:, z * span - left : (z + 1) * span - left].T
                for x in range(NX):
                    put_dense(out_ref, seat(z, x), update[x * rows : (x + 1) * rows])
                seats = pl.ds(seat(z, 0), NX)
                sent.append(pltpu.make_async_copy(out_ref.at[seats], out_hbm.at[seats], sems.at[z]))
                sent[-1].start()
    for copy in sent + [keep]:
        copy.wait()


def muon_step(owned, rows, momentum_t):
    columns, total_rows = momentum_t.shape
    scale = 0.2 * math.sqrt(max(columns, total_rows))
    square = pltpu.VMEM((columns, columns), jnp.bfloat16)
    return pl.pallas_call(
        functools.partial(step_kernel, scale),
        out_shape=(
            jax.ShapeDtypeStruct(rows.shape, jnp.bfloat16),
            jax.ShapeDtypeStruct(momentum_t.shape, jnp.bfloat16),
        ),
        in_specs=[SMEM, VMEM, VMEM],
        out_specs=(HBM, HBM),
        scratch_shapes=[
            pltpu.VMEM(momentum_t.shape, jnp.float32),
            pltpu.VMEM(momentum_t.shape, jnp.bfloat16),
            square,
            square,
            pltpu.VMEM(momentum_t.shape, jnp.bfloat16),
            pltpu.VMEM(rows.shape, jnp.bfloat16),
            pltpu.SemaphoreType.DMA,
            pltpu.SemaphoreType.DMA((NZ,)),
        ],
        compiler_params=pltpu.CompilerParams(vmem_limit_bytes=24 * 2**20),
        name="newton_schulz",
    )(owned, rows, momentum_t)


def select_kernel(seats, order, counts, where, blocks, out):
    group = where[0]

    def body(k, carry):
        out[k] = blocks[seats[order[group * SHARDS + k]]]
        return carry

    lax.fori_loop(0, counts[group], body, 0)


def select(seats, order, counts, where, blocks, slots):
    return pl.pallas_call(
        select_kernel,
        out_shape=jax.ShapeDtypeStruct((slots,) + blocks.shape[1:], blocks.dtype),
        in_specs=[SMEM] * 4 + [VMEM],
        out_specs=VMEM,
        compiler_params=pltpu.CompilerParams(vmem_limit_bytes=16 * 2**20),
        name="select_blocks",
    )(seats, order, counts, where, blocks)


def place_kernel(origins, order, counts, where, *refs):
    pieces, (out, rows, sems) = refs[: len(origins)], refs[-3:]
    height = out.shape[1]
    offsets = [sum(piece.shape[0] for piece in pieces[:i]) for i in range(len(pieces))]

    def unpack(chosen, k, carry):
        for i in chosen:
            for tile, value in enumerate(get_dense(pieces[i], k, height)):
                left = tile * LANES
                rows[offsets[i] + k, :, left : left + value.shape[1]] = value
        return carry

    homes = [((where[0] ^ core) + NC * hop) & (GROUPS - 1) for core, hop, _ in origins]

    def copy(i, k):
        m = order[homes[i] * SHARDS + origins[i][2] + k]
        return pltpu.make_async_copy(rows.at[offsets[i] + k], out.at[m], sems.at[m])

    def start(chosen, k, carry):
        unpack(chosen, k, carry)
        for i in chosen:
            pl.when(origins[i][2] + k < counts[homes[i]])(lambda i=i: copy(i, k).start())
        return carry

    done = 0
    for size in sorted({piece.shape[0] for piece in pieces}):
        chosen = [i for i, piece in enumerate(pieces) if piece.shape[0] >= size]
        lax.fori_loop(done, size, functools.partial(start, chosen), 0)
        done = size

    for i, piece in enumerate(pieces):

        def wait(k, carry, i=i):
            copy(i, k).wait()
            return carry

        lax.fori_loop(0, jnp.minimum(counts[homes[i]] - origins[i][2], piece.shape[0]), wait, 0)


def place(origins, order, counts, where, pieces, shape, base=None):
    bases = [] if base is None else [base]
    slots = sum(piece.shape[0] for piece in pieces)
    return pl.pallas_call(
        functools.partial(place_kernel, origins),
        out_shape=jax.ShapeDtypeStruct(shape, pieces[0].dtype),
        in_specs=[SMEM] * 3 + [VMEM] * len(pieces) + [HBM] * len(bases),
        out_specs=HBM,
        input_output_aliases={3 + len(pieces): 0} if bases else {},
        scratch_shapes=[
            pltpu.VMEM((slots,) + shape[1:], pieces[0].dtype),
            pltpu.SemaphoreType.DMA((shape[0],)),
        ],
        compiler_params=pltpu.CompilerParams(vmem_limit_bytes=16 * 2**20),
        name="place_blocks",
    )(order, counts, where, *pieces, *bases)


def spread(slots, shape, seats, order, counts, where, blocks):
    split = (slots + 1) // 2
    own = select(seats, order, counts, where, blocks, slots)
    low, high = own[:split], own[split:]
    below_low, above_high = hop_y(low, 1), hop_y(high, -1)
    below_high, above_low = hop_y(high, 1), hop_y(low, -1)
    far = [hop_y(below_low, 1), hop_y(above_high, -1)]
    def at(core, origins):
        return [(core, *origin) for origin in origins]

    tables = (order, counts, where)
    early = lax.optimization_barrier([own, below_low, above_high])
    early_origins = [(0, 0), (3, 0), (1, split)]
    late_origins = [(3, split), (1, 0), (2, 0), (2, split)]
    updates = place(at(0, early_origins), *tables, early, shape)
    updates, *late = lax.optimization_barrier([updates, below_high, above_low] + far)
    early_other = [hop_core(piece) for piece in early]
    late_other = [hop_core(piece) for piece in late]
    origins = at(1, early_origins) + at(0, late_origins)
    updates = place(origins, *tables, early_other + late, shape, updates)
    return place(at(1, late_origins), *tables, late_other, shape, updates)


def on_device(grads, momentum, owners):
    count = owners.shape[0]
    group = lax.axis_index("dp")
    me = lax.axis_index(AXES)
    where = group[None].astype(jnp.int32)
    packed = pack(owners, where, grads)
    rows = lax.all_to_all(packed, AXES, 0, 0, tiled=True, axis_index_groups=MEMBERS)

    ids = jnp.arange(count, dtype=jnp.int32)
    homes = owners // SHARDS
    seats = seat((owners >> 2) & (NZ - 1), owners & (NX - 1))
    before = (homes[:, None] == homes[None, :]) & (owners[None, :] < owners[:, None])
    slot = homes * SHARDS + jnp.sum(before.astype(jnp.int32), axis=1)
    order = jnp.sum(
        jnp.where(slot[None, :] == jnp.arange(GROUPS * SHARDS, dtype=jnp.int32)[:, None], ids[None, :], 0), axis=1
    )
    counts = jnp.sum((homes[None, :] == jnp.arange(GROUPS, dtype=jnp.int32)[:, None]).astype(jnp.int32), axis=1)
    owned = jnp.any(owners == me)[None].astype(jnp.int32)

    blocks, following = muon_step(owned, rows, momentum[0].T)
    blocks = lax.all_to_all(blocks, AXES, 0, 0, tiled=True, axis_index_groups=MEMBERS)
    few = 19
    updates = lax.cond(
        jnp.max(counts) <= few,
        functools.partial(spread, few, grads.shape),
        functools.partial(spread, SHARDS, grads.shape),
        seats,
        order,
        counts,
        where,
        blocks,
    )
    return (updates, following.T[None])


def solution(mesh):
    return jax.shard_map(
        on_device,
        mesh=mesh,
        in_specs=(P(None, "shard", None), P(AXES, None, None), P()),
        out_specs=(P(None, "shard", None), P(AXES, None, None)),
        check_vma=False,
    )
```
